256 devices in a mesh: acq: 32 (over z, y), az: 8 (over x, core).
Axes of the slice: x: 4, y: 4, z: 8, core: 2. Of those that a mesh axis runs over, the one named last changes fastest.
Arguments:
- slc_re: float32 [192, 80, 1280], P('acq', 'az')
- slc_im: float32 [192, 80, 1280], P('acq', 'az')
- pairs: int32 [512, 2], P('acq'), may hold values from 0 to 191, as said below
Outputs:
- coherence: float32 [512, 16, 64], P('acq', 'az')
- ifg_re: float32 [512, 16, 64], P('acq', 'az')
- ifg_im: float32 [512, 16, 64], P('acq', 'az')
The draws below stay inside these ranges and needn't reach their ends.
Inputs may be any that keep to these rules, and one draw needn't show every extreme that they name: `pairs`: rows d * 16 to (d + 1) * 16 - 1 have their reference acquisition among d * 6 to (d + 1) * 6 - 1. Within such a block of rows, the secondaries taken from any one aligned group of 6 acquisitions are all the same acquisition. A pair's two acquisitions differ.
All inputs are finite; a program needn't handle non-finite values.
Results may differ from the reference program's by a relative error of at most 0.00002.
Values sent between devices are 32-bit elements; how exact they have to be, the bound alone decides.
No kernel may reach another device: no remote copies, remote signals or barrier semaphores. Data moves between devices by JAX's collectives and lax.ppermute only.
A program may use at most 128 MiB of HBM per device.

```python
import math
import jax
import jax.numpy as jnp
from jax import lax

ACQ_DEV = 6
PAIR_DEV = 16
RG = 1280
ACQ = 192
AZ = 80


def scene_parts(key, row_top):
    key = jax.random.fold_in(key, 11)
    key_scene_re, key_scene_im, key_spread, key_noise_re, key_noise_im, key_rows = jax.random.split(key, 6)
    scene_re = jax.random.normal(key_scene_re, (1, AZ, RG), jnp.float32)
    scene_im = jax.random.normal(key_scene_im, (1, AZ, RG), jnp.float32)
    spread = jnp.exp(jax.random.uniform(key_spread, (ACQ, AZ, RG), jnp.float32, math.log(0.3), math.log(3.0)))
    noise_re = jax.random.normal(key_noise_re, (ACQ, AZ, RG), jnp.float32)
    noise_im = jax.random.normal(key_noise_im, (ACQ, AZ, RG), jnp.float32)
    row_scale = jnp.exp(jax.random.uniform(key_rows, (1, AZ, 1), jnp.float32, 0.0, math.log(row_top)))
    return (row_scale * (scene_re + spread * noise_re), row_scale * (scene_im + spread * noise_im))


def draw_slc_re(key, part):
    row_top = 1.0
    return scene_parts(key, row_top)[0]


def draw_slc_im(key, part):
    row_top = 1.0
    return scene_parts(key, row_top)[1]


def draw_pairs(key, part):
    key = jax.random.fold_in(key, 7)
    groups = ACQ // ACQ_DEV
    key_chosen, key_source, key_offset = jax.random.split(key, 3)
    chosen = jax.random.randint(key_chosen, (groups, groups), 0, ACQ_DEV)
    source = jax.random.randint(key_source, (groups, PAIR_DEV), 0, groups)
    offset_draw = jax.random.randint(key_offset, (groups, PAIR_DEV), 1, ACQ_DEV)
    group_ids = jnp.arange(groups)
    own_pick = chosen[group_ids, group_ids][:, None]
    first_acq = group_ids[:, None] * ACQ_DEV + (own_pick + offset_draw) % ACQ_DEV
    second = source * ACQ_DEV + jnp.take_along_axis(chosen, source, axis=1)
    return jnp.stack([first_acq, second], axis=-1).reshape(groups * PAIR_DEV, 2).astype(jnp.int32)


def setup_inputs(seed: int = 0) -> dict:
    splits = jax.random.split(jax.random.key(seed), 4)
    slc_re = draw_slc_re(jax.random.fold_in(splits[3], 71), 0)
    slc_im = draw_slc_im(jax.random.fold_in(splits[3], 71), 0)
    pairs = draw_pairs(jax.random.fold_in(splits[3], 71), 0)
    return dict(slc_re=slc_re, slc_im=slc_im, pairs=pairs)


def cross_terms(anchor, partner):
    anchor_re = anchor[..., 0, :, :]
    anchor_im = anchor[..., 1, :, :]
    partner_re = partner[..., 0, :, :]
    partner_im = partner[..., 1, :, :]
    return jnp.stack([anchor_re * partner_re + anchor_im * partner_im, anchor_im * partner_re - anchor_re * partner_im, anchor_re * anchor_re + anchor_im * anchor_im, partner_re * partner_re + partner_im * partner_im], axis=-3)

def range_box(values):
    width = values.shape[-1]
    padded = jnp.pad(values, [(0, 0)] * (values.ndim - 1) + [(10, 9)])
    sum_two = padded[..., :-1] + padded[..., 1:]
    sum_four = sum_two[..., :-2] + sum_two[..., 2:]
    sum_eight = sum_four[..., :-4] + sum_four[..., 4:]
    sum_sixteen = sum_eight[..., :-8] + sum_eight[..., 8:]
    return sum_sixteen[..., :width] + sum_four[..., 16:16 + width]

def azimuth_box(values, height):
    summed = values[..., 0:height, :]
    for offset in range(1, 5):
        summed = summed + values[..., offset:offset + height, :]
    return summed

def look_sum(values):
    height = values.shape[-2]
    width = values.shape[-1]
    shaped = values.reshape(values.shape[:-2] + (height // 5, 5, width // 20, 20))
    return lax.optimization_barrier(jnp.sum(shaped, axis=(-3, -1)))

def finish(direct, window):
    magnitude = jnp.sqrt(window[..., 0, :, :] ** 2 + window[..., 1, :, :] ** 2)
    local_coh = magnitude / jnp.sqrt(window[..., 2, :, :] * window[..., 3, :, :] + 1e-06)
    coherence = look_sum(local_coh) / 100.0
    looked = look_sum(direct)
    scale_look = jnp.sqrt(looked[..., 2, :, :] * looked[..., 3, :, :] + 1e-06)
    return (coherence, looked[..., 0, :, :] / scale_look, looked[..., 1, :, :] / scale_look)

def reference(slc_re, slc_im, pairs):
    acq_tiles = jnp.stack([slc_re, slc_im], axis=1)

    def one_pair(pair_row):
        anchor = acq_tiles[pair_row[0]]
        partner = acq_tiles[pair_row[1]]
        direct = cross_terms(anchor, partner)
        ranged = range_box(direct)
        padded = jnp.pad(ranged, ((0, 0), (2, 2), (0, 0)))
        window = azimuth_box(padded, AZ)
        return finish(direct, window)
    coherence, ifg_re, ifg_im = lax.map(one_pair, pairs)
    return (coherence, ifg_re, ifg_im)
```

```python
import jax
import jax.numpy as jnp
from jax import lax
from jax.experimental import pallas as pl
from jax.experimental.pallas import tpu as pltpu
from jax.sharding import PartitionSpec as P

DEVS = 32
ACQ_DEV = 6
ACQ = DEVS * ACQ_DEV
PAIR_DEV = 16
PAIRS = DEVS * PAIR_DEV
ROWS = 10
HALF = 5
RG = 1280
STEP = 40
WIDE = STEP + 19
CHUNK = 60
K = 256
F32 = jnp.float32
BF16 = jnp.bfloat16
VMEM = pl.BlockSpec(memory_space=pltpu.VMEM)
HBM = pl.BlockSpec(memory_space=pltpu.HBM)
BIG = 3.38e38
PART = 8 * ACQ_DEV


def lanes_of(shape):
    return lax.broadcasted_iota(jnp.int32, shape, len(shape) - 1)


def pack_kernel(re_hbm, im_hbm, pairs_hbm, out_ref, re_ref, im_ref, pairs_ref, sems):
    copies = [
        pltpu.make_async_copy(source, target, sems.at[n])
        for n, (source, target) in enumerate(((pairs_hbm, pairs_ref), (re_hbm, re_ref), (im_hbm, im_ref)))
    ]
    for copy in copies:
        copy.start()
    lane = lanes_of((ACQ_DEV, 128))
    wide = lanes_of((PAIR_DEV, 128))
    copies[0].wait()
    acq = pairs_ref[...]
    group = (acq * 171) >> 10
    local = (acq - ACQ_DEV * group) * 8 + (group & 7)
    order = lax.broadcasted_iota(jnp.int32, (2, PAIR_DEV), 0)
    index = (local + jnp.where(order == 0, 0, (group >> 3) * PART)).astype(F32)
    square = (PAIR_DEV, PAIR_DEV)
    diagonal = lax.broadcasted_iota(jnp.int32, square, 0) == lax.broadcasted_iota(jnp.int32, square, 1)
    columns = [
        jnp.sum(jnp.where(diagonal, jnp.broadcast_to(index[w : w + 1, :], square), 0.0), axis=1, keepdims=True)
        for w in range(2)
    ]
    first, second = [jnp.broadcast_to(column, (PAIR_DEV, 128)) for column in columns]
    for part, ref in enumerate((re_ref, im_ref)):
        copies[1 + part].wait()
        for r in range(HALF):
            for d in range(DEVS):
                start = STEP * d - 10
                k = start // 128
                off = start - 128 * k
                halves = []
                for row, base in ((r, 0), (r + HALF, 64)):
                    shift = (base - off) % 128
                    pieces = []
                    for t in (k, k + 1):
                        if 0 <= t < RG // 128 and (t == k or off + WIDE > 128):
                            x = ref[row, :, t * 128 : (t + 1) * 128]
                            pieces.append(pltpu.roll(x, shift, 1) if shift else x)
                        else:
                            pieces.append(jnp.zeros((ACQ_DEV, 128), F32))
                    if off + WIDE > 128:
                        halves.append(jnp.where(lane < base + 128 - off, pieces[0], pieces[1]))
                    else:
                        halves.append(pieces[0])
                top = d * CHUNK + (part * HALF + r) * ACQ_DEV
                both = jnp.where(lane < 64, halves[0], halves[1])
                out_ref[top : top + ACQ_DEV, :] = jnp.where((lane & 63) < WIDE, both, 0.0)
    for d in range(DEVS):
        head = out_ref[d * CHUNK : d * CHUNK + PAIR_DEV, :]
        head = jnp.where(wide == 60, first, jnp.where(wide == 61, second, head))
        out_ref[d * CHUNK : d * CHUNK + PAIR_DEV, :] = head


def acq_rows(recv_ref, part, r):
    base = (part * HALF + r) * ACQ_DEV
    return jnp.concatenate(
        [recv_ref[pl.ds(base + a + 8 * g * CHUNK, 8, stride=CHUNK), :] for g in range(4) for a in range(ACQ_DEV)],
        axis=0,
    )


def edges_kernel(recv_ref, low_ref, high_ref):
    lane = lanes_of((ACQ, 128))
    for part in range(2):
        rows = [acq_rows(recv_ref, part, r) for r in (0, 1, 3, 4)]
        low_ref[part * ACQ : (part + 1) * ACQ, :] = jnp.where(lane < 64, rows[0], pltpu.roll(rows[1], 64, 1))
        high_ref[part * ACQ : (part + 1) * ACQ, :] = jnp.where(lane < 64, pltpu.roll(rows[2], 64, 1), rows[3])


def pieces_of(x, count):
    out = []
    for n in range(count):
        piece = x.astype(BF16)
        out.append(piece)
        if n + 1 < count:
            x = x - piece.astype(F32)
    return out


def clamp(x):
    return jnp.minimum(jnp.maximum(x, -BIG), BIG)


def dot(x, y):
    return jnp.dot(x, y, preferred_element_type=F32)


def fill(table):
    for p in range(3):
        table[p * K + ACQ : (p + 1) * K, :] = jnp.zeros((K - ACQ, table.shape[1]), BF16)


def enter(table, x, at):
    for p, piece in enumerate(pieces_of(clamp(x), 3)):
        table[p * K : p * K + ACQ, at : at + x.shape[1]] = piece


def along_range():
    shape = (128, 128)
    k = lax.broadcasted_iota(jnp.int32, shape, 0)
    n = lax.broadcasted_iota(jnp.int32, shape, 1)
    c = n & 63
    first = jnp.where(c < STEP, c, jnp.where(c < STEP + 4, 10 + 20 * (c & 1), -1000))
    sample = k & 63
    inside = ((k >> 6) == (n >> 6)) & (sample >= first) & (sample <= first + 19)
    box = jnp.where(inside, 1.0, 0.0).astype(BF16)
    return jnp.concatenate([box, box], axis=0)


def choose(pick_a, pick_b, table, picked, at, width):
    columns = slice(at, at + width)
    picked[PAIRS:, columns] = dot(pick_b[...], table[:, columns])
    for g in range(4):
        few = jnp.concatenate([table[p * K + g * PART : p * K + (g + 1) * PART, columns] for p in range(3)], axis=0)
        picked[128 * g : 128 * (g + 1), columns] = dot(pick_a[128 * g : 128 * (g + 1), : 3 * PART], few)


def cross(picked, top, count):
    fields = [[], []]
    for t in range(count):
        ra = picked[pl.ds(top, 16), t * 256 : t * 256 + 128]
        ia = picked[pl.ds(top, 16), t * 256 + 128 : t * 256 + 256]
        rb = picked[pl.ds(top + PAIRS, 16), t * 256 : t * 256 + 128]
        ib = picked[pl.ds(top + PAIRS, 16), t * 256 + 128 : t * 256 + 256]
        fields[0].append(ra * rb + ia * ib)
        fields[1].append(ia * rb - ra * ib)
    return fields


def own_rows(v):
    v0, v1, v2, v3, v4 = v
    low = lanes_of(v0.shape) < 64
    v12, v34 = v1 + v2, v3 + v4
    v012, v234 = v0 + v12, v2 + v34
    return [
        v012 + jnp.where(low, 0.0, pltpu.roll(v34, 64, 1)),
        (v012 + v3) + jnp.where(low, 0.0, pltpu.roll(v4, 64, 1)),
        v012 + v34,
        (v1 + v234) + jnp.where(low, pltpu.roll(v0, 64, 1), 0.0),
        v234 + jnp.where(low, pltpu.roll(v0 + v1, 64, 1), 0.0),
    ]


def edge_rows(v, up, down):
    low = lanes_of(up.shape) < 64
    up_turned, down_turned = pltpu.roll(up, 64, 1), pltpu.roll(down, 64, 1)
    return [
        v[0] + jnp.where(low, up + up_turned, 0.0),
        v[1] + jnp.where(low, up_turned, 0.0),
        v[2],
        v[3] + jnp.where(low, 0.0, down_turned),
        v[4] + jnp.where(low, 0.0, down + down_turned),
    ]


def own_kernel(recv_ref, sums_ref, power_ref, pick_a, pick_b, table, picked):
    lane = lanes_of((128, K))
    few = lane - PART * ((lane * 342) >> 14)
    for g in range(4):
        head = jnp.concatenate([recv_ref[pl.ds(8 * g * CHUNK + p, 8, stride=CHUNK), :] for p in range(PAIR_DEV)], axis=0)
        rows = slice(128 * g, 128 * (g + 1))
        index = jnp.broadcast_to(head[:, 60:61], (128, K))
        pick_a[rows, :] = jnp.where(index == few.astype(F32), 1.0, 0.0).astype(BF16)
        index = jnp.broadcast_to(head[:, 61:62], (128, K))
        hot = jnp.where(index == lane.astype(F32), 1.0, 0.0).astype(BF16)
        for p in range(3):
            pick_b[rows, p * K : (p + 1) * K] = hot
    fill(table)
    squares = []
    for t in range(HALF):
        parts = [acq_rows(recv_ref, part, t) for part in range(2)]
        for part, x in enumerate(parts):
            enter(table, x, t * 256 + part * 128)
        squares.append(parts[0] * parts[0] + parts[1] * parts[1])
        choose(pick_a, pick_b, table, picked, t * 256, 256)
    for r, x in enumerate(own_rows(squares)):
        power_ref[:, r * 128 : (r + 1) * 128] = x

    def some(g, carry):
        top = pl.multiple_of(16 * g, 16)
        for f, field in enumerate(cross(picked, top, HALF)):
            for r, x in enumerate(own_rows(field)):
                sums_ref[pl.ds(top + f * PAIRS, 16), r * 128 : (r + 1) * 128] = x
        return carry

    lax.fori_loop(0, PAIRS // 16, some, 0, unroll=True)


def pair_kernel(up_ref, down_ref, sums_ref, power_ref, pick_a, pick_b, out_ref, table, picked, terms, total, ends):
    fill(table)
    box = along_range()
    squares = []
    for t, ref in enumerate((up_ref, down_ref)):
        parts = [ref[part * ACQ : (part + 1) * ACQ, :] for part in range(2)]
        for part, x in enumerate(parts):
            enter(table, x, t * 256 + part * 128)
        squares.append(parts[0] * parts[0] + parts[1] * parts[1])
        choose(pick_a, pick_b, table, picked, t * 256, 256)
    own = [power_ref[:, r * 128 : (r + 1) * 128] for r in range(HALF)]
    for r, x in enumerate(edge_rows(own, *squares)):
        enter(table, dot(jnp.concatenate(pieces_of(x, 2), axis=1), box), 512 + r * 128)
    choose(pick_a, pick_b, table, picked, 512, 640)

    def rows(g, carry):
        top = pl.multiple_of(16 * g, 16)
        for f, field in enumerate(cross(picked, top, 2)):
            own = [sums_ref[pl.ds(top + f * PAIRS, 16), r * 128 : (r + 1) * 128] for r in range(HALF)]
            for r, x in enumerate(edge_rows(own, *field)):
                for n, piece in enumerate(pieces_of(x, 2)):
                    terms[pl.ds(top + (2 * r + f) * PAIRS, 16), n * 128 : (n + 1) * 128] = piece
        return carry

    lax.fori_loop(0, PAIRS // 16, rows, 0, unroll=True)
    total[...] = dot(terms[...], box)

    lane = lanes_of((16, 128)) & 63

    def some(g, carry):
        top = pl.multiple_of(16 * g, 16)
        coherence = None
        for r in range(HALF):
            x0 = total[pl.ds(top + 2 * r * PAIRS, 16), :]
            x1 = total[pl.ds(top + (2 * r + 1) * PAIRS, 16), :]
            wa = picked[pl.ds(top, 16), 512 + r * 128 : 640 + r * 128]
            wb = picked[pl.ds(top + PAIRS, 16), 512 + r * 128 : 640 + r * 128]
            inverse = lax.rsqrt(wa * wb + 1e-06)
            num = x0 * x0 + x1 * x1
            size = num * lax.rsqrt(jnp.maximum(num, 1e-37)) * inverse
            coherence = size if coherence is None else coherence + size
            if r == 2:
                look = jnp.where(lane < STEP + 2, x0, x1) * inverse
        value = jnp.where(lane < STEP, coherence, look)
        for p, piece in enumerate(pieces_of(value, 3)):
            ends[pl.ds(top, 16), p * 128 : (p + 1) * 128] = piece
        return carry

    lax.fori_loop(0, PAIRS // 16, some, 0, unroll=True)

    n = lax.broadcasted_iota(jnp.int32, (128, 256), 0)
    m = lax.broadcasted_iota(jnp.int32, (128, 256), 1)
    c, j, o = n & 63, m >> 7, (m >> 5) & 3
    first = jnp.where(o == 0, 20 * j, jnp.where(o == 3, 1000, STEP - 2 + 2 * o + j))
    last = first + jnp.where(o == 0, 19, 0)
    same = ((n >> 6) == (m & 1)) & (c >= first) & (c <= last)
    spread = jnp.where(same, 1.0, 0.0).astype(BF16)
    result = dot(ends[...], jnp.concatenate([spread] * 3, axis=0))
    owner = (lanes_of((8, 128)) >> 1) & 15
    for j in range(2):
        for g in range(4):
            out = None
            for p in range(PAIR_DEV):
                top = 128 * g + 8 * p
                rows_p = result[top : top + 8, j * 128 : (j + 1) * 128]
                out = rows_p if out is None else jnp.where(owner == p, rows_p, out)
            out_ref[pl.ds(16 * g + j, 8, stride=2), :] = out


def finish_kernel(got_ref, coh_ref, re_ref, im_ref):
    turned = jnp.transpose(got_ref[...])
    coh_ref[...] = turned[0:32] * 0.01
    re_ref[...] = turned[32:64]
    im_ref[...] = turned[64:96]


def call(kernel, outs, specs, scratch=(), limit=40, **more):
    return pl.pallas_call(
        kernel,
        out_shape=outs,
        in_specs=specs,
        out_specs=jax.tree.map(lambda _: VMEM, outs),
        scratch_shapes=[pltpu.VMEM(*x) if isinstance(x, tuple) else x for x in scratch],
        compiler_params=pltpu.CompilerParams(vmem_limit_bytes=limit * 1024 * 1024),
        **more,
    )


def f32(*shape):
    return jax.ShapeDtypeStruct(shape, F32)


def bf16(*shape):
    return jax.ShapeDtypeStruct(shape, BF16)


OWN_OUTS = (f32(2 * PAIRS, HALF * 128), f32(ACQ, HALF * 128), bf16(PAIRS, K), bf16(PAIRS, 3 * K))
OWN_SCRATCH = (((3 * K, HALF * 256), BF16), ((2 * PAIRS, HALF * 256), F32))
PAIR_SCRATCH = (
    ((3 * K, 512 + HALF * 128), BF16),
    ((2 * PAIRS, 512 + HALF * 128), F32),
    ((2 * HALF * PAIRS, 256), BF16),
    ((2 * HALF * PAIRS, 128), F32),
    ((PAIRS, 3 * 128), BF16),
)


def per_device(slc_re, slc_im, pairs):
    send = call(
        pack_kernel,
        f32(DEVS * CHUNK, 128),
        [HBM] * 3,
        (
            ((ROWS, ACQ_DEV, RG), F32),
            ((ROWS, ACQ_DEV, RG), F32),
            ((2, PAIR_DEV), jnp.int32),
            pltpu.SemaphoreType.DMA((3,)),
        ),
        limit=60,
    )(jnp.transpose(slc_re, (1, 0, 2)), jnp.transpose(slc_im, (1, 0, 2)), pairs.T)
    send = send.reshape(DEVS, CHUNK // 4, 4, 128)
    recv = lax.all_to_all(send, "acq", split_axis=0, concat_axis=0, tiled=True)
    recv = recv.reshape(DEVS * CHUNK, 128)
    low, high = call(edges_kernel, (f32(2 * ACQ, 128), f32(2 * ACQ, 128)), [VMEM])(recv)
    ends = lax.axis_size("az") - 1
    up = lax.ppermute(high, "az", [(i, i + 1) for i in range(ends)])
    down = lax.ppermute(low, "az", [(i + 1, i) for i in range(ends)])
    cost = pl.CostEstimate(flops=5 * 10**9, bytes_accessed=10**7, transcendentals=0)
    partial = call(own_kernel, OWN_OUTS, [VMEM], OWN_SCRATCH, cost_estimate=cost)(recv)
    result = call(pair_kernel, f32(2 * DEVS, 128), [VMEM] * 6, PAIR_SCRATCH)(up, down, *partial)
    got = lax.all_to_all(result.reshape(DEVS, 2, 128), "acq", split_axis=0, concat_axis=0, tiled=True)
    outs = call(finish_kernel, (f32(32, 64),) * 3, [VMEM])(got.reshape(2 * DEVS, 128))
    return tuple(x.reshape(PAIR_DEV, 2, 64) for x in outs)


def solution(mesh):
    in_specs = (P("acq", "az", None), P("acq", "az", None), P("acq", None))
    out_specs = (P("acq", "az", None), P("acq", "az", None), P("acq", "az", None))
    return jax.shard_map(per_device, mesh=mesh, in_specs=in_specs, out_specs=out_specs, check_vma=False)
```

```python
import jax
import jax.numpy as jnp
from jax import lax
from jax.experimental import pallas as pl
from jax.experimental.pallas import tpu as pltpu
from jax.sharding import PartitionSpec as P

DEVS = 32
ACQ_DEV = 6
ACQ = DEVS * ACQ_DEV
PAIR_DEV = 16
PAIRS = DEVS * PAIR_DEV
ROWS = 10
HALF = 5
RG = 1280
STEP = 40
WIDE = STEP + 19
CHUNK = 60
K = 256
F32 = jnp.float32
BF16 = jnp.bfloat16
VMEM = pl.BlockSpec(memory_space=pltpu.VMEM)
HBM = pl.BlockSpec(memory_space=pltpu.HBM)
BIG = 3.38e38
PART = 8 * ACQ_DEV


def lanes_of(shape):
    return lax.broadcasted_iota(jnp.int32, shape, len(shape) - 1)


def pack_kernel(re_hbm, im_hbm, pairs_hbm, out_ref, re_ref, im_ref, pairs_ref, sems):
    copies = [
        pltpu.make_async_copy(source, target, sems.at[n])
        for n, (source, target) in enumerate(((pairs_hbm, pairs_ref), (re_hbm, re_ref), (im_hbm, im_ref)))
    ]
    for copy in copies:
        copy.start()
    lane = lanes_of((ACQ_DEV, 128))
    wide = lanes_of((PAIR_DEV, 128))
    copies[0].wait()
    acq = pairs_ref[...]
    group = (acq * 171) >> 10
    local = (acq - ACQ_DEV * group) * 8 + (group & 7)
    order = lax.broadcasted_iota(jnp.int32, (2, PAIR_DEV), 0)
    index = (local + jnp.where(order == 0, 0, (group >> 3) * PART)).astype(F32)
    square = (PAIR_DEV, PAIR_DEV)
    diagonal = lax.broadcasted_iota(jnp.int32, square, 0) == lax.broadcasted_iota(jnp.int32, square, 1)
    columns = [
        jnp.sum(jnp.where(diagonal, jnp.broadcast_to(index[w : w + 1, :], square), 0.0), axis=1, keepdims=True)
        for w in range(2)
    ]
    first, second = [jnp.broadcast_to(column, (PAIR_DEV, 128)) for column in columns]
    for part, ref in enumerate((re_ref, im_ref)):
        copies[1 + part].wait()
        for r in range(HALF):
            for d in range(DEVS):
                start = STEP * d - 10
                k = start // 128
                off = start - 128 * k
                halves = []
                for row, base in ((r, 0), (r + HALF, 64)):
                    shift = (base - off) % 128
                    pieces = []
                    for t in (k, k + 1):
                        if 0 <= t < RG // 128 and (t == k or off + WIDE > 128):
                            x = ref[row, :, t * 128 : (t + 1) * 128]
                            pieces.append(pltpu.roll(x, shift, 1) if shift else x)
                        else:
                            pieces.append(jnp.zeros((ACQ_DEV, 128), F32))
                    if off + WIDE > 128:
                        halves.append(jnp.where(lane < base + 128 - off, pieces[0], pieces[1]))
                    else:
                        halves.append(pieces[0])
                top = d * CHUNK + (part * HALF + r) * ACQ_DEV
                both = jnp.where(lane < 64, halves[0], halves[1])
                out_ref[top : top + ACQ_DEV, :] = jnp.where((lane & 63) < WIDE, both, 0.0)
    for d in range(DEVS):
        head = out_ref[d * CHUNK : d * CHUNK + PAIR_DEV, :]
        head = jnp.where(wide == 60, first, jnp.where(wide == 61, second, head))
        out_ref[d * CHUNK : d * CHUNK + PAIR_DEV, :] = head


def acq_rows(recv_ref, part, r):
    base = (part * HALF + r) * ACQ_DEV
    return jnp.concatenate(
        [recv_ref[pl.ds(base + a + 8 * g * CHUNK, 8, stride=CHUNK), :] for g in range(4) for a in range(ACQ_DEV)],
        axis=0,
    )


def odd_row():
    return lax.axis_index("az") & 1


def edges_kernel(recv_ref, chip_ref, core_ref):
    lane = lanes_of((ACQ, 128))
    odd = odd_row() == 1
    for part in range(2):
        rows = [acq_rows(recv_ref, part, r) for r in (0, 1, 3, 4)]
        low = jnp.where(lane < 64, rows[0], pltpu.roll(rows[1], 64, 1))
        high = jnp.where(lane < 64, pltpu.roll(rows[2], 64, 1), rows[3])
        chip_ref[part * ACQ : (part + 1) * ACQ, :] = jnp.where(odd, high, low)
        core_ref[part * ACQ : (part + 1) * ACQ, :] = jnp.where(odd, low, high)


def pieces_of(x, count):
    out = []
    for n in range(count):
        piece = x.astype(BF16)
        out.append(piece)
        if n + 1 < count:
            x = x - piece.astype(F32)
    return out


def clamp(x):
    return jnp.minimum(jnp.maximum(x, -BIG), BIG)


def dot(x, y):
    return jnp.dot(x, y, preferred_element_type=F32)


def fill(table):
    for p in range(3):
        table[p * K + ACQ : (p + 1) * K, :] = jnp.zeros((K - ACQ, table.shape[1]), BF16)


def enter(table, x, at):
    for p, piece in enumerate(pieces_of(clamp(x), 3)):
        table[p * K : p * K + ACQ, at : at + x.shape[1]] = piece


def along_range():
    shape = (128, 128)
    k = lax.broadcasted_iota(jnp.int32, shape, 0)
    n = lax.broadcasted_iota(jnp.int32, shape, 1)
    c = n & 63
    first = jnp.where(c < STEP, c, jnp.where(c < STEP + 4, 10 + 20 * (c & 1), -1000))
    sample = k & 63
    inside = ((k >> 6) == (n >> 6)) & (sample >= first) & (sample <= first + 19)
    box = jnp.where(inside, 1.0, 0.0).astype(BF16)
    return jnp.concatenate([box, box], axis=0)


def choose(pick_a, pick_b, table, picked, at, width):
    columns = slice(at, at + width)
    picked[PAIRS:, columns] = dot(pick_b[...], table[:, columns])
    for g in range(4):
        few = jnp.concatenate([table[p * K + g * PART : p * K + (g + 1) * PART, columns] for p in range(3)], axis=0)
        picked[128 * g : 128 * (g + 1), columns] = dot(pick_a[128 * g : 128 * (g + 1), : 3 * PART], few)


def cross(picked, top, count):
    fields = [[], []]
    for t in range(count):
        ra = picked[pl.ds(top, 16), t * 256 : t * 256 + 128]
        ia = picked[pl.ds(top, 16), t * 256 + 128 : t * 256 + 256]
        rb = picked[pl.ds(top + PAIRS, 16), t * 256 : t * 256 + 128]
        ib = picked[pl.ds(top + PAIRS, 16), t * 256 + 128 : t * 256 + 256]
        fields[0].append(ra * rb + ia * ib)
        fields[1].append(ia * rb - ra * ib)
    return fields


def own_rows(v):
    v0, v1, v2, v3, v4 = v
    low = lanes_of(v0.shape) < 64
    v12, v34 = v1 + v2, v3 + v4
    v012, v234 = v0 + v12, v2 + v34
    return [
        v012 + jnp.where(low, 0.0, pltpu.roll(v34, 64, 1)),
        (v012 + v3) + jnp.where(low, 0.0, pltpu.roll(v4, 64, 1)),
        v012 + v34,
        (v1 + v234) + jnp.where(low, pltpu.roll(v0, 64, 1), 0.0),
        v234 + jnp.where(low, pltpu.roll(v0 + v1, 64, 1), 0.0),
    ]


def edge_rows(v, up, down):
    low = lanes_of(up.shape) < 64
    up_turned, down_turned = pltpu.roll(up, 64, 1), pltpu.roll(down, 64, 1)
    return [
        v[0] + jnp.where(low, up + up_turned, 0.0),
        v[1] + jnp.where(low, up_turned, 0.0),
        v[2],
        v[3] + jnp.where(low, 0.0, down_turned),
        v[4] + jnp.where(low, 0.0, down + down_turned),
    ]


def own_kernel(recv_ref, sums_ref, power_ref, pick_a, pick_b, table, picked):
    lane = lanes_of((128, K))
    few = lane - PART * ((lane * 342) >> 14)
    for g in range(4):
        head = jnp.concatenate([recv_ref[pl.ds(8 * g * CHUNK + p, 8, stride=CHUNK), :] for p in range(PAIR_DEV)], axis=0)
        rows = slice(128 * g, 128 * (g + 1))
        index = jnp.broadcast_to(head[:, 60:61], (128, K))
        pick_a[rows, :] = jnp.where(index == few.astype(F32), 1.0, 0.0).astype(BF16)
        index = jnp.broadcast_to(head[:, 61:62], (128, K))
        hot = jnp.where(index == lane.astype(F32), 1.0, 0.0).astype(BF16)
        for p in range(3):
            pick_b[rows, p * K : (p + 1) * K] = hot
    fill(table)
    squares = []
    for t in range(HALF):
        parts = [acq_rows(recv_ref, part, t) for part in range(2)]
        for part, x in enumerate(parts):
            enter(table, x, t * 256 + part * 128)
        squares.append(parts[0] * parts[0] + parts[1] * parts[1])
        choose(pick_a, pick_b, table, picked, t * 256, 256)
    for r, x in enumerate(own_rows(squares)):
        power_ref[:, r * 128 : (r + 1) * 128] = x

    def some(g, carry):
        top = pl.multiple_of(16 * g, 16)
        for f, field in enumerate(cross(picked, top, HALF)):
            for r, x in enumerate(own_rows(field)):
                sums_ref[pl.ds(top + f * PAIRS, 16), r * 128 : (r + 1) * 128] = x
        return carry

    lax.fori_loop(0, PAIRS // 16, some, 0, unroll=True)


def pair_kernel(chip_ref, core_ref, sums_ref, power_ref, pick_a, pick_b, out_ref, table, picked, terms, total, ends):
    fill(table)
    box = along_range()
    squares = []
    odd = odd_row() == 1
    for t, (even_ref, odd_ref) in enumerate(((chip_ref, core_ref), (core_ref, chip_ref))):
        at = [slice(part * ACQ, (part + 1) * ACQ) for part in range(2)]
        parts = [jnp.where(odd, odd_ref[rows, :], even_ref[rows, :]) for rows in at]
        for part, x in enumerate(parts):
            enter(table, x, t * 256 + part * 128)
        squares.append(parts[0] * parts[0] + parts[1] * parts[1])
        choose(pick_a, pick_b, table, picked, t * 256, 256)
    own = [power_ref[:, r * 128 : (r + 1) * 128] for r in range(HALF)]
    for r, x in enumerate(edge_rows(own, *squares)):
        enter(table, dot(jnp.concatenate(pieces_of(x, 2), axis=1), box), 512 + r * 128)
    choose(pick_a, pick_b, table, picked, 512, 640)

    def rows(g, carry):
        top = pl.multiple_of(16 * g, 16)
        for f, field in enumerate(cross(picked, top, 2)):
            own = [sums_ref[pl.ds(top + f * PAIRS, 16), r * 128 : (r + 1) * 128] for r in range(HALF)]
            for r, x in enumerate(edge_rows(own, *field)):
                for n, piece in enumerate(pieces_of(x, 2)):
                    terms[pl.ds(top + (2 * r + f) * PAIRS, 16), n * 128 : (n + 1) * 128] = piece
        return carry

    lax.fori_loop(0, PAIRS // 16, rows, 0, unroll=True)
    total[...] = dot(terms[...], box)

    lane = lanes_of((16, 128)) & 63

    def some(g, carry):
        top = pl.multiple_of(16 * g, 16)
        coherence = None
        for r in range(HALF):
            x0 = total[pl.ds(top + 2 * r * PAIRS, 16), :]
            x1 = total[pl.ds(top + (2 * r + 1) * PAIRS, 16), :]
            wa = picked[pl.ds(top, 16), 512 + r * 128 : 640 + r * 128]
            wb = picked[pl.ds(top + PAIRS, 16), 512 + r * 128 : 640 + r * 128]
            inverse = lax.rsqrt(wa * wb + 1e-06)
            num = x0 * x0 + x1 * x1
            size = num * lax.rsqrt(jnp.maximum(num, 1e-37)) * inverse
            coherence = size if coherence is None else coherence + size
            if r == 2:
                look = jnp.where(lane < STEP + 2, x0, x1) * inverse
        value = jnp.where(lane < STEP, coherence, look)
        for p, piece in enumerate(pieces_of(value, 3)):
            ends[pl.ds(top, 16), p * 128 : (p + 1) * 128] = piece
        return carry

    lax.fori_loop(0, PAIRS // 16, some, 0, unroll=True)

    n = lax.broadcasted_iota(jnp.int32, (128, 256), 0)
    m = lax.broadcasted_iota(jnp.int32, (128, 256), 1)
    c, j, o = n & 63, m >> 7, (m >> 5) & 3
    first = jnp.where(o == 0, 20 * j, jnp.where(o == 3, 1000, STEP - 2 + 2 * o + j))
    last = first + jnp.where(o == 0, 19, 0)
    same = ((n >> 6) == (m & 1)) & (c >= first) & (c <= last)
    spread = jnp.where(same, 1.0, 0.0).astype(BF16)
    result = dot(ends[...], jnp.concatenate([spread] * 3, axis=0))
    owner = (lanes_of((8, 128)) >> 1) & 15
    for j in range(2):
        for g in range(4):
            out = None
            for p in range(PAIR_DEV):
                top = 128 * g + 8 * p
                rows_p = result[top : top + 8, j * 128 : (j + 1) * 128]
                out = rows_p if out is None else jnp.where(owner == p, rows_p, out)
            out_ref[pl.ds(16 * g + j, 8, stride=2), :] = out


def finish_kernel(got_ref, coh_ref, re_ref, im_ref):
    turned = jnp.transpose(got_ref[...])
    coh_ref[...] = turned[0:32] * 0.01
    re_ref[...] = turned[32:64]
    im_ref[...] = turned[64:96]


def call(kernel, outs, specs, scratch=(), limit=40, **more):
    return pl.pallas_call(
        kernel,
        out_shape=outs,
        in_specs=specs,
        out_specs=jax.tree.map(lambda _: VMEM, outs),
        scratch_shapes=[pltpu.VMEM(*x) if isinstance(x, tuple) else x for x in scratch],
        compiler_params=pltpu.CompilerParams(vmem_limit_bytes=limit * 1024 * 1024),
        **more,
    )


def f32(*shape):
    return jax.ShapeDtypeStruct(shape, F32)


def bf16(*shape):
    return jax.ShapeDtypeStruct(shape, BF16)


OWN_OUTS = (f32(2 * PAIRS, HALF * 128), f32(ACQ, HALF * 128), bf16(PAIRS, K), bf16(PAIRS, 3 * K))
OWN_SCRATCH = (((3 * K, HALF * 256), BF16), ((2 * PAIRS, HALF * 256), F32))
PAIR_SCRATCH = (
    ((3 * K, 512 + HALF * 128), BF16),
    ((2 * PAIRS, 512 + HALF * 128), F32),
    ((2 * HALF * PAIRS, 256), BF16),
    ((2 * HALF * PAIRS, 128), F32),
    ((PAIRS, 3 * 128), BF16),
)


def per_device(slc_re, slc_im, pairs):
    send = call(
        pack_kernel,
        f32(DEVS * CHUNK, 128),
        [HBM] * 3,
        (
            ((ROWS, ACQ_DEV, RG), F32),
            ((ROWS, ACQ_DEV, RG), F32),
            ((2, PAIR_DEV), jnp.int32),
            pltpu.SemaphoreType.DMA((3,)),
        ),
        limit=60,
    )(jnp.transpose(slc_re, (1, 0, 2)), jnp.transpose(slc_im, (1, 0, 2)), pairs.T)
    send = send.reshape(DEVS, CHUNK // 4, 4, 128)
    recv = lax.all_to_all(send, "acq", split_axis=0, concat_axis=0, tiled=True)
    recv = recv.reshape(DEVS * CHUNK, 128)
    chip, core = call(edges_kernel, (f32(2 * ACQ, 128), f32(2 * ACQ, 128)), [VMEM])(recv)
    count = lax.axis_size("az")
    across = [(i, i + 1) for i in range(1, count - 1, 2)]
    inside = [(i, i + 1) for i in range(0, count, 2)]
    chip = lax.ppermute(chip, "az", across + [(j, i) for i, j in across])
    core = lax.ppermute(core, "az", inside + [(j, i) for i, j in inside])
    cost = pl.CostEstimate(flops=5 * 10**9, bytes_accessed=10**7, transcendentals=0)
    partial = call(own_kernel, OWN_OUTS, [VMEM], OWN_SCRATCH, cost_estimate=cost)(recv)
    result = call(pair_kernel, f32(2 * DEVS, 128), [VMEM] * 6, PAIR_SCRATCH)(chip, core, *partial)
    got = lax.all_to_all(result.reshape(DEVS, 2, 128), "acq", split_axis=0, concat_axis=0, tiled=True)
    outs = call(finish_kernel, (f32(32, 64),) * 3, [VMEM])(got.reshape(2 * DEVS, 128))
    return tuple(x.reshape(PAIR_DEV, 2, 64) for x in outs)


def solution(mesh):
    in_specs = (P("acq", "az", None), P("acq", "az", None), P("acq", None))
    out_specs = (P("acq", "az", None), P("acq", "az", None), P("acq", "az", None))
    return jax.shard_map(per_device, mesh=mesh, in_specs=in_specs, out_specs=out_specs, check_vma=False)
```

```python
import jax
import jax.numpy as jnp
from jax import lax
from jax.experimental import pallas as pl
from jax.experimental.pallas import tpu as pltpu
from jax.sharding import PartitionSpec as P

DEVS = 32
ACQ_DEV = 6
ACQ = DEVS * ACQ_DEV
PAIR_DEV = 16
PAIRS = DEVS * PAIR_DEV
ROWS = 10
HALF = 5
RG = 1280
STEP = 40
WIDE = STEP + 19
CHUNK = 60
K = 256
F32 = jnp.float32
BF16 = jnp.bfloat16
VMEM = pl.BlockSpec(memory_space=pltpu.VMEM)
HBM = pl.BlockSpec(memory_space=pltpu.HBM)
BIG = 3.38e38
PART = 8 * ACQ_DEV


def lanes_of(shape):
    return lax.broadcasted_iota(jnp.int32, shape, len(shape) - 1)


def odd_row():
    return lax.axis_index("az") & 1


def pack_kernel(re_hbm, im_hbm, pairs_hbm, out_hbm, re_ref, im_ref, pairs_ref, later, chunks, sems):
    odd = odd_row()
    copies = [
        pltpu.make_async_copy(source, target, sems.at[n])
        for n, (source, target) in enumerate(((pairs_hbm, pairs_ref), (re_hbm, re_ref), (im_hbm, im_ref)))
    ]
    for copy in copies:
        copy.start()
    lane = lanes_of((ACQ_DEV, 128))
    wide = lanes_of((PAIR_DEV, 128))
    copies[0].wait()
    acq = pairs_ref[...]
    group = (acq * 171) >> 10
    local = (acq - ACQ_DEV * group) * 8 + (group & 7)
    order = lax.broadcasted_iota(jnp.int32, (2, PAIR_DEV), 0)
    index = (local + jnp.where(order == 0, 0, (group >> 3) * PART)).astype(F32)
    square = (PAIR_DEV, PAIR_DEV)
    diagonal = lax.broadcasted_iota(jnp.int32, square, 0) == lax.broadcasted_iota(jnp.int32, square, 1)
    columns = [
        jnp.sum(jnp.where(diagonal, jnp.broadcast_to(index[w : w + 1, :], square), 0.0), axis=1, keepdims=True)
        for w in range(2)
    ]
    first, second = [jnp.broadcast_to(column, (PAIR_DEV, 128)) for column in columns]
    tiles = RG // 128
    for part, ref in enumerate((re_ref, im_ref)):
        copies[1 + part].wait()
        for r in range(HALF):
            row = r + HALF + odd * (9 - 2 * (r + HALF))
            for t in range(tiles):
                x = ref[row, :, t * 128 : (t + 1) * 128]
                later[part * HALF + r, :, t * 128 : (t + 1) * 128] = pltpu.roll(x, 64, 1)
    out_copies = []
    for d in range(DEVS):
        start = STEP * d - 10
        k = start // 128
        off = start - 128 * k
        spans = []
        for t, low, high in ((k, off, min(128, off + WIDE)), (k + 1, 0, off + WIDE - 128)):
            if low < high and 0 <= t < tiles:
                spans.append((t, False, low, high))
                shifted = [(low + 64, min(high + 64, 128)), (max(low + 64, 128) - 128, high + 64 - 128)]
                spans += [(t, True, x, y) for x, y in shifted if x < y]
        masks = [(lane >= low) & (lane < high) for _, _, low, high in spans]
        for part, ref in enumerate((re_ref, im_ref)):
            for r in range(HALF):
                row = r + odd * (9 - 2 * r)
                mixed = jnp.zeros((ACQ_DEV, 128), F32)
                for (t, shifted, _, _), mask in zip(spans, masks):
                    at = slice(t * 128, (t + 1) * 128)
                    mixed = jnp.where(mask, later[part * HALF + r, :, at] if shifted else ref[row, :, at], mixed)
                top = d * CHUNK + (part * HALF + r) * ACQ_DEV
                chunks[top : top + ACQ_DEV, :] = pltpu.roll(mixed, 128 - off, 1) if off else mixed
        head = chunks[d * CHUNK : d * CHUNK + PAIR_DEV, :]
        head = jnp.where(wide == 60, first, jnp.where(wide == 61, second, head))
        chunks[d * CHUNK : d * CHUNK + PAIR_DEV, :] = head
        if d % 8 == 7:
            rows = pl.ds((d - 7) * CHUNK, 8 * CHUNK)
            out_copies.append(pltpu.make_async_copy(chunks.at[rows, :], out_hbm.at[rows, :], sems.at[3 + d // 8]))
            out_copies[-1].start()
    for copy in out_copies:
        copy.wait()


def acq_rows(recv_ref, part, r):
    base = (part * HALF + r) * ACQ_DEV
    return jnp.concatenate(
        [recv_ref[pl.ds(base + a + 8 * g * CHUNK, 8, stride=CHUNK), :] for g in range(4) for a in range(ACQ_DEV)],
        axis=0,
    )


def edges_kernel(recv_ref, chip_ref, core_ref):
    lane = lanes_of((ACQ, 128))
    for part in range(2):
        v0, v1, v3, v4 = [acq_rows(recv_ref, part, r) for r in (0, 1, 3, 4)]
        rows = slice(part * ACQ, (part + 1) * ACQ)
        chip_ref[rows, :] = jnp.where(lane < 64, v0, pltpu.roll(v1, 64, 1))
        core_ref[rows, :] = jnp.where(lane < 64, pltpu.roll(v3, 64, 1), v4)
    chip_ref[2 * ACQ :, :] = jnp.zeros((8, 128), F32)


def pieces_of(x, count):
    out = []
    for n in range(count):
        piece = x.astype(BF16)
        out.append(piece)
        if n + 1 < count:
            x = x - piece.astype(F32)
    return out


def clamp(x):
    return jnp.minimum(jnp.maximum(x, -BIG), BIG)


def dot(x, y):
    return jnp.dot(x, y, preferred_element_type=F32)


def fill(table):
    for p in range(3):
        table[p * K + ACQ : (p + 1) * K, :] = jnp.zeros((K - ACQ, table.shape[1]), BF16)


def enter(table, x, at):
    for p, piece in enumerate(pieces_of(clamp(x), 3)):
        table[p * K : p * K + ACQ, at : at + x.shape[1]] = piece


def along_range():
    shape = (128, 128)
    k = lax.broadcasted_iota(jnp.int32, shape, 0)
    n = lax.broadcasted_iota(jnp.int32, shape, 1)
    c = n & 63
    first = jnp.where(c < STEP, c, jnp.where(c < STEP + 4, 10 + 20 * (c & 1), -1000))
    sample = k & 63
    inside = ((k >> 6) == (n >> 6)) & (sample >= first) & (sample <= first + 19)
    box = jnp.where(inside, 1.0, 0.0).astype(BF16)
    return jnp.concatenate([box, box], axis=0)


def choose(pick_a, pick_b, table, picked, at, width):
    columns = slice(at, at + width)
    picked[PAIRS:, columns] = dot(pick_b[...], table[:, columns])
    for g in range(4):
        few = jnp.concatenate([table[p * K + g * PART : p * K + (g + 1) * PART, columns] for p in range(3)], axis=0)
        picked[128 * g : 128 * (g + 1), columns] = dot(pick_a[128 * g : 128 * (g + 1), : 3 * PART], few)


def cross(picked, top, count):
    fields = [[], []]
    for t in range(count):
        ra = picked[pl.ds(top, 16), t * 256 : t * 256 + 128]
        ia = picked[pl.ds(top, 16), t * 256 + 128 : t * 256 + 256]
        rb = picked[pl.ds(top + PAIRS, 16), t * 256 : t * 256 + 128]
        ib = picked[pl.ds(top + PAIRS, 16), t * 256 + 128 : t * 256 + 256]
        fields[0].append(ra * rb + ia * ib)
        fields[1].append(ia * rb - ra * ib)
    return fields


def own_rows(v):
    v0, v1, v2, v3, v4 = v
    low = lanes_of(v0.shape) < 64
    next_one = pltpu.roll(jnp.where(low, v4, v0), 64, 1)
    next_two = next_one + pltpu.roll(jnp.where(low, v3, v1), 64, 1)
    v12, v34 = v1 + v2, v3 + v4
    v012, v234 = v0 + v12, v2 + v34
    return [
        v012 + jnp.where(low, 0.0, next_two),
        (v012 + v3) + jnp.where(low, 0.0, next_one),
        v012 + v34,
        (v1 + v234) + jnp.where(low, next_one, 0.0),
        v234 + jnp.where(low, next_two, 0.0),
    ]


def edge_rows(near, far, edge, low):
    inside = (lanes_of(edge.shape) < 64) == low
    return near + jnp.where(inside, edge + pltpu.roll(edge, 64, 1), 0.0), far + jnp.where(inside, edge, 0.0)


def store_terms(terms, top, x):
    for n, piece in enumerate(pieces_of(x, 2)):
        terms[pl.ds(top, 16), n * 128 : (n + 1) * 128] = piece


def enter_power(table, x, box, at):
    enter(table, dot(jnp.concatenate(pieces_of(x, 2), axis=1), box), at)


def coherence_of(total, picked, top, row, at):
    x0 = total[pl.ds(top + 2 * row * PAIRS, 16), :]
    x1 = total[pl.ds(top + (2 * row + 1) * PAIRS, 16), :]
    wa = picked[pl.ds(top, 16), at : at + 128]
    wb = picked[pl.ds(top + PAIRS, 16), at : at + 128]
    inverse = lax.rsqrt(wa * wb + 1e-06)
    num = x0 * x0 + x1 * x1
    return num * lax.rsqrt(jnp.maximum(num, 1e-37)) * inverse, x0, x1, inverse


def for_pairs(body):
    def step(g, carry):
        body(pl.multiple_of(16 * g, 16))
        return carry

    lax.fori_loop(0, PAIRS // 16, step, 0, unroll=True)


def own_kernel(
    recv_ref, up_ref, down_ref, up_power, down_power, pick_a, pick_b, value_ref, table, picked, terms, total
):
    lane = lanes_of((128, K))
    few = lane - PART * ((lane * 342) >> 14)
    for g in range(4):
        head = jnp.concatenate([recv_ref[pl.ds(8 * g * CHUNK + p, 8, stride=CHUNK), :] for p in range(PAIR_DEV)], axis=0)
        rows = slice(128 * g, 128 * (g + 1))
        index = jnp.broadcast_to(head[:, 60:61], (128, K))
        pick_a[rows, :] = jnp.where(index == few.astype(F32), 1.0, 0.0).astype(BF16)
        index = jnp.broadcast_to(head[:, 61:62], (128, K))
        hot = jnp.where(index == lane.astype(F32), 1.0, 0.0).astype(BF16)
        for p in range(3):
            pick_b[rows, p * K : (p + 1) * K] = hot
    fill(table)
    box = along_range()
    squares = []
    for t in range(HALF):
        parts = [acq_rows(recv_ref, part, t) for part in range(2)]
        for part, x in enumerate(parts):
            enter(table, x, t * 256 + part * 128)
        squares.append(parts[0] * parts[0] + parts[1] * parts[1])
        choose(pick_a, pick_b, table, picked, t * 256, 256)
    sums = own_rows(squares)
    up_power[:, 0:128], up_power[:, 128:256] = sums[0], sums[1]
    down_power[:, 0:128], down_power[:, 128:256] = sums[4], sums[3]
    enter_power(table, sums[2], box, HALF * 256)
    choose(pick_a, pick_b, table, picked, HALF * 256, 128)

    def rows(top):
        for f, field in enumerate(cross(picked, top, HALF)):
            x = own_rows(field)
            here = pl.ds(top + f * PAIRS, 16)
            up_ref[here, 0:128], up_ref[here, 128:256] = x[0], x[1]
            down_ref[here, 0:128], down_ref[here, 128:256] = x[4], x[3]
            store_terms(terms, top + f * PAIRS, x[2])

    for_pairs(rows)
    total[...] = dot(terms[...], box)
    lane16 = lanes_of((16, 128)) & 63

    def some(top):
        size, x0, x1, inverse = coherence_of(total, picked, top, 0, HALF * 256)
        value_ref[pl.ds(top, 16), :] = jnp.where(lane16 < STEP, size, jnp.where(lane16 < STEP + 2, x0, x1) * inverse)

    for_pairs(some)


def edge_coherence(edge_ref, sums_ref, power_ref, pick_a, pick_b, table, picked, terms, total, low):
    fill(table)
    box = along_range()
    parts = [edge_ref[part * ACQ : (part + 1) * ACQ, :] for part in range(2)]
    for part, x in enumerate(parts):
        enter(table, x, part * 128)
    choose(pick_a, pick_b, table, picked, 0, 256)
    square = parts[0] * parts[0] + parts[1] * parts[1]
    for n, x in enumerate(edge_rows(power_ref[:, 0:128], power_ref[:, 128:256], square, low)):
        enter_power(table, x, box, 256 + n * 128)
    choose(pick_a, pick_b, table, picked, 256, 256)

    def rows(top):
        for f, field in enumerate(cross(picked, top, 1)):
            here = pl.ds(top + f * PAIRS, 16)
            for n, x in enumerate(edge_rows(sums_ref[here, 0:128], sums_ref[here, 128:256], field[0], low)):
                store_terms(terms, top + (2 * n + f) * PAIRS, x)

    for_pairs(rows)
    total[...] = dot(terms[...], box)


def edge_value(value_ref, total, picked, top):
    size = coherence_of(total, picked, top, 0, 256)[0] + coherence_of(total, picked, top, 1, 384)[0]
    return value_ref[pl.ds(top, 16), :] + jnp.where((lanes_of(size.shape) & 63) < STEP, size, 0.0)


def core_kernel(core_ref, sums_ref, power_ref, pick_a, pick_b, value_ref, out_ref, table, picked, terms, total):
    edge_coherence(core_ref, sums_ref, power_ref, pick_a, pick_b, table, picked, terms, total, False)

    def some(top):
        out_ref[pl.ds(top, 16), :] = edge_value(value_ref, total, picked, top)

    for_pairs(some)


def chip_kernel(chip_ref, sums_ref, power_ref, pick_a, pick_b, value_ref, out_ref, table, picked, terms, total, ends):
    edge_coherence(chip_ref, sums_ref, power_ref, pick_a, pick_b, table, picked, terms, total, True)

    def some(top):
        for p, piece in enumerate(pieces_of(edge_value(value_ref, total, picked, top), 3)):
            ends[pl.ds(top, 16), p * 128 : (p + 1) * 128] = piece

    for_pairs(some)

    n = lax.broadcasted_iota(jnp.int32, (128, 256), 0)
    m = lax.broadcasted_iota(jnp.int32, (128, 256), 1)
    c, j, o = n & 63, m >> 7, (m >> 5) & 3
    first = jnp.where(o == 0, 20 * j, jnp.where(o == 3, 1000, STEP - 2 + 2 * o + j))
    last = first + jnp.where(o == 0, 19, 0)
    same = ((n >> 6) == ((m & 1) ^ odd_row())) & (c >= first) & (c <= last)
    spread = jnp.where(same, 1.0, 0.0).astype(BF16)
    result = dot(ends[...], jnp.concatenate([spread] * 3, axis=0))
    owner = (lanes_of((8, 128)) >> 1) & 15
    for j in range(2):
        for g in range(4):
            out = None
            for p in range(PAIR_DEV):
                top = 128 * g + 8 * p
                rows_p = result[top : top + 8, j * 128 : (j + 1) * 128]
                out = rows_p if out is None else jnp.where(owner == p, rows_p, out)
            out_ref[pl.ds(16 * g + j, 8, stride=2), :] = out


def finish_kernel(got_ref, coh_ref, re_ref, im_ref):
    turned = jnp.transpose(got_ref[...])
    coh_ref[...] = turned[0:32] * 0.01
    re_ref[...] = turned[32:64]
    im_ref[...] = turned[64:96]


def call(kernel, outs, specs, scratch=(), limit=40, out_spec=VMEM, **more):
    return pl.pallas_call(
        kernel,
        out_shape=outs,
        in_specs=specs,
        out_specs=jax.tree.map(lambda _: out_spec, outs),
        scratch_shapes=[pltpu.VMEM(*x) if isinstance(x, tuple) else x for x in scratch],
        compiler_params=pltpu.CompilerParams(vmem_limit_bytes=limit * 1024 * 1024),
        **more,
    )


def f32(*shape):
    return jax.ShapeDtypeStruct(shape, F32)


def bf16(*shape):
    return jax.ShapeDtypeStruct(shape, BF16)


EDGE_OUTS = (f32(2 * PAIRS, 256),) * 2 + (f32(ACQ, 256),) * 2
OWN_OUTS = EDGE_OUTS + (bf16(PAIRS, K), bf16(PAIRS, 3 * K), f32(PAIRS, 128))
OWN_SCRATCH = (
    ((3 * K, HALF * 256 + 128), BF16),
    ((2 * PAIRS, HALF * 256 + 128), F32),
    ((2 * PAIRS, 256), BF16),
    ((2 * PAIRS, 128), F32),
)
EDGE_SCRATCH = (
    ((3 * K, 512), BF16),
    ((2 * PAIRS, 512), F32),
    ((4 * PAIRS, 256), BF16),
    ((4 * PAIRS, 128), F32),
)
CHIP_SCRATCH = EDGE_SCRATCH + (((PAIRS, 3 * 128), BF16),)


def per_device(slc_re, slc_im, pairs):
    send = call(
        pack_kernel,
        f32(DEVS * CHUNK, 128),
        [HBM] * 3,
        (
            ((ROWS, ACQ_DEV, RG), F32),
            ((ROWS, ACQ_DEV, RG), F32),
            ((2, PAIR_DEV), jnp.int32),
            ((2 * HALF, ACQ_DEV, RG), F32),
            ((DEVS * CHUNK, 128), F32),
            pltpu.SemaphoreType.DMA((7,)),
        ),
        limit=60,
        out_spec=HBM,
    )(jnp.transpose(slc_re, (1, 0, 2)), jnp.transpose(slc_im, (1, 0, 2)), pairs.T)
    send = send.reshape(DEVS, CHUNK // 4, 4, 128)
    recv = lax.all_to_all(send, "acq", split_axis=0, concat_axis=0, tiled=True)
    recv = recv.reshape(DEVS * CHUNK, 128)
    chip, core = call(edges_kernel, (f32(2 * ACQ + 8, 128), f32(2 * ACQ, 128)), [VMEM])(recv)
    count = lax.axis_size("az")
    across = [(i, i + 1) for i in range(1, count - 1, 2)]
    inside = [(i, i + 1) for i in range(0, count, 2)]
    chip = lax.ppermute(chip, "az", across + [(j, i) for i, j in across])
    core = lax.ppermute(core, "az", inside + [(j, i) for i, j in inside])
    cost = [pl.CostEstimate(flops=n, bytes_accessed=n, transcendentals=0) for n in (10**3, 10**3)]
    own = call(own_kernel, OWN_OUTS, [VMEM], OWN_SCRATCH, cost_estimate=cost[0])(recv)
    up, down, up_power, down_power, pick_a, pick_b, value = own
    value = call(core_kernel, f32(PAIRS, 128), [VMEM] * 6, EDGE_SCRATCH, cost_estimate=cost[1])(
        core, down, down_power, pick_a, pick_b, value
    )
    result = call(chip_kernel, f32(2 * DEVS, 128), [VMEM] * 6, CHIP_SCRATCH)(
        chip, up, up_power, pick_a, pick_b, value
    )
    got = lax.all_to_all(result.reshape(DEVS, 2, 128), "acq", split_axis=0, concat_axis=0, tiled=True)
    outs = call(finish_kernel, (f32(32, 64),) * 3, [VMEM])(got.reshape(2 * DEVS, 128))
    return tuple(x.reshape(PAIR_DEV, 2, 64) for x in outs)


def solution(mesh):
    in_specs = (P("acq", "az", None), P("acq", "az", None), P("acq", None))
    out_specs = (P("acq", "az", None), P("acq", "az", None), P("acq", "az", None))
    return jax.shard_map(per_device, mesh=mesh, in_specs=in_specs, out_specs=out_specs, check_vma=False)
```

```python
import jax
import jax.numpy as jnp
from jax import lax
from jax.experimental import pallas as pl
from jax.experimental.pallas import tpu as pltpu
from jax.sharding import PartitionSpec as P

DEVS = 32
ACQ_DEV = 6
ACQ = DEVS * ACQ_DEV
PAIR_DEV = 16
PAIRS = DEVS * PAIR_DEV
ROWS = 10
HALF = 5
RG = 1280
STEP = 40
WIDE = STEP + 19
CHUNK = 60
K = 256
F32 = jnp.float32
BF16 = jnp.bfloat16
VMEM = pl.BlockSpec(memory_space=pltpu.VMEM)
HBM = pl.BlockSpec(memory_space=pltpu.HBM)
BIG = 3.38e38
PART = 8 * ACQ_DEV


def lanes_of(shape):
    return lax.broadcasted_iota(jnp.int32, shape, len(shape) - 1)


def odd_row():
    return lax.axis_index("az") & 1


def pack_kernel(re_hbm, im_hbm, pairs_hbm, chunks, re_ref, im_ref, pairs_ref, later, sems):
    odd = odd_row()
    copies = [
        pltpu.make_async_copy(source, target, sems.at[n])
        for n, (source, target) in enumerate(((pairs_hbm, pairs_ref), (re_hbm, re_ref), (im_hbm, im_ref)))
    ]
    for copy in copies:
        copy.start()
    lane = lanes_of((ACQ_DEV, 128))
    wide = lanes_of((PAIR_DEV, 128))
    copies[0].wait()
    acq = pairs_ref[...]
    group = (acq * 171) >> 10
    local = (acq - ACQ_DEV * group) * 8 + (group & 7)
    order = lax.broadcasted_iota(jnp.int32, (2, PAIR_DEV), 0)
    index = (local + jnp.where(order == 0, 0, (group >> 3) * PART)).astype(F32)
    square = (PAIR_DEV, PAIR_DEV)
    diagonal = lax.broadcasted_iota(jnp.int32, square, 0) == lax.broadcasted_iota(jnp.int32, square, 1)
    columns = [
        jnp.sum(jnp.where(diagonal, jnp.broadcast_to(index[w : w + 1, :], square), 0.0), axis=1, keepdims=True)
        for w in range(2)
    ]
    first, second = [jnp.broadcast_to(column, (PAIR_DEV, 128)) for column in columns]
    tiles = RG // 128
    for part, ref in enumerate((re_ref, im_ref)):
        copies[1 + part].wait()
        for r in range(HALF):
            row = r + HALF + odd * (9 - 2 * (r + HALF))
            for t in range(tiles):
                x = ref[row, :, t * 128 : (t + 1) * 128]
                later[part * HALF + r, :, t * 128 : (t + 1) * 128] = pltpu.roll(x, 64, 1)
    for d in range(DEVS):
        start = STEP * d - 10
        k = start // 128
        off = start - 128 * k
        spans = []
        for t, low, high in ((k, off, min(128, off + WIDE)), (k + 1, 0, off + WIDE - 128)):
            if low < high and 0 <= t < tiles:
                spans.append((t, False, low, high))
                shifted = [(low + 64, min(high + 64, 128)), (max(low + 64, 128) - 128, high + 64 - 128)]
                spans += [(t, True, x, y) for x, y in shifted if x < y]
        masks = [(lane >= low) & (lane < high) for _, _, low, high in spans]
        for part, ref in enumerate((re_ref, im_ref)):
            for r in range(HALF):
                row = r + odd * (9 - 2 * r)
                mixed = jnp.zeros((ACQ_DEV, 128), F32)
                for (t, shifted, _, _), mask in zip(spans, masks):
                    at = slice(t * 128, (t + 1) * 128)
                    mixed = jnp.where(mask, later[part * HALF + r, :, at] if shifted else ref[row, :, at], mixed)
                top = d * CHUNK + (part * HALF + r) * ACQ_DEV
                chunks[top : top + ACQ_DEV, :] = pltpu.roll(mixed, 128 - off, 1) if off else mixed
        head = chunks[d * CHUNK : d * CHUNK + PAIR_DEV, :]
        head = jnp.where(wide == 60, first, jnp.where(wide == 61, second, head))
        chunks[d * CHUNK : d * CHUNK + PAIR_DEV, :] = head


def acq_rows(recv_ref, part, r):
    base = (part * HALF + r) * ACQ_DEV
    return jnp.concatenate(
        [recv_ref[pl.ds(base + a + 8 * g * CHUNK, 8, stride=CHUNK), :] for g in range(4) for a in range(ACQ_DEV)],
        axis=0,
    )


def edges_kernel(recv_ref, chip_ref, core_ref):
    lane = lanes_of((ACQ, 128))
    for part in range(2):
        v0, v1, v3, v4 = [acq_rows(recv_ref, part, r) for r in (0, 1, 3, 4)]
        rows = slice(part * ACQ, (part + 1) * ACQ)
        chip_ref[rows, :] = jnp.where(lane < 64, v0, pltpu.roll(v1, 64, 1))
        core_ref[rows, :] = jnp.where(lane < 64, pltpu.roll(v3, 64, 1), v4)
    chip_ref[2 * ACQ :, :] = jnp.zeros((8, 128), F32)


def pieces_of(x, count):
    out = []
    for n in range(count):
        piece = x.astype(BF16)
        out.append(piece)
        if n + 1 < count:
            x = x - piece.astype(F32)
    return out


def clamp(x):
    return jnp.minimum(jnp.maximum(x, -BIG), BIG)


def dot(x, y):
    return jnp.dot(x, y, preferred_element_type=F32)


def fill(table):
    for p in range(3):
        table[p * K + ACQ : (p + 1) * K, :] = jnp.zeros((K - ACQ, table.shape[1]), BF16)


def enter(table, x, at):
    for p, piece in enumerate(pieces_of(clamp(x), 3)):
        table[p * K : p * K + ACQ, at : at + x.shape[1]] = piece


def along_range():
    shape = (128, 128)
    k = lax.broadcasted_iota(jnp.int32, shape, 0)
    n = lax.broadcasted_iota(jnp.int32, shape, 1)
    c = n & 63
    first = jnp.where(c < STEP, c, jnp.where(c < STEP + 4, 10 + 20 * (c & 1), -1000))
    sample = k & 63
    inside = ((k >> 6) == (n >> 6)) & (sample >= first) & (sample <= first + 19)
    box = jnp.where(inside, 1.0, 0.0).astype(BF16)
    return jnp.concatenate([box, box], axis=0)


def choose(pick_a, pick_b, table, picked, at, width):
    columns = slice(at, at + width)
    picked[PAIRS:, columns] = dot(pick_b[...], table[:, columns])
    for g in range(4):
        few = jnp.concatenate([table[p * K + g * PART : p * K + (g + 1) * PART, columns] for p in range(3)], axis=0)
        picked[128 * g : 128 * (g + 1), columns] = dot(pick_a[128 * g : 128 * (g + 1), : 3 * PART], few)


def cross(picked, top, count):
    fields = [[], []]
    for t in range(count):
        ra = picked[pl.ds(top, 16), t * 256 : t * 256 + 128]
        ia = picked[pl.ds(top, 16), t * 256 + 128 : t * 256 + 256]
        rb = picked[pl.ds(top + PAIRS, 16), t * 256 : t * 256 + 128]
        ib = picked[pl.ds(top + PAIRS, 16), t * 256 + 128 : t * 256 + 256]
        fields[0].append(ra * rb + ia * ib)
        fields[1].append(ia * rb - ra * ib)
    return fields


def own_rows(v):
    v0, v1, v2, v3, v4 = v
    low = lanes_of(v0.shape) < 64
    next_one = pltpu.roll(jnp.where(low, v4, v0), 64, 1)
    next_two = next_one + pltpu.roll(jnp.where(low, v3, v1), 64, 1)
    v12, v34 = v1 + v2, v3 + v4
    v012, v234 = v0 + v12, v2 + v34
    return [
        v012 + jnp.where(low, 0.0, next_two),
        (v012 + v3) + jnp.where(low, 0.0, next_one),
        v012 + v34,
        (v1 + v234) + jnp.where(low, next_one, 0.0),
        v234 + jnp.where(low, next_two, 0.0),
    ]


def edge_rows(near, far, edge, low):
    inside = (lanes_of(edge.shape) < 64) == low
    return near + jnp.where(inside, edge + pltpu.roll(edge, 64, 1), 0.0), far + jnp.where(inside, edge, 0.0)


def store_terms(terms, top, x):
    for n, piece in enumerate(pieces_of(x, 2)):
        terms[pl.ds(top, 16), n * 128 : (n + 1) * 128] = piece


def enter_power(table, x, box, at):
    enter(table, dot(jnp.concatenate(pieces_of(x, 2), axis=1), box), at)


def coherence_of(total, picked, top, row, at):
    x0 = total[pl.ds(top + 2 * row * PAIRS, 16), :]
    x1 = total[pl.ds(top + (2 * row + 1) * PAIRS, 16), :]
    wa = picked[pl.ds(top, 16), at : at + 128]
    wb = picked[pl.ds(top + PAIRS, 16), at : at + 128]
    inverse = lax.rsqrt(wa * wb + 1e-06)
    num = x0 * x0 + x1 * x1
    return num * lax.rsqrt(jnp.maximum(num, 1e-37)) * inverse, x0, x1, inverse


def for_pairs(body):
    def step(g, carry):
        body(pl.multiple_of(16 * g, 16))
        return carry

    lax.fori_loop(0, PAIRS // 16, step, 0, unroll=True)


def own_kernel(
    recv_ref, up_ref, down_ref, up_power, down_power, pick_a, pick_b, value_ref, table, picked, terms, total
):
    lane = lanes_of((128, K))
    few = lane - PART * ((lane * 342) >> 14)
    for g in range(4):
        head = jnp.concatenate([recv_ref[pl.ds(8 * g * CHUNK + p, 8, stride=CHUNK), :] for p in range(PAIR_DEV)], axis=0)
        rows = slice(128 * g, 128 * (g + 1))
        index = jnp.broadcast_to(head[:, 60:61], (128, K))
        pick_a[rows, :] = jnp.where(index == few.astype(F32), 1.0, 0.0).astype(BF16)
        index = jnp.broadcast_to(head[:, 61:62], (128, K))
        hot = jnp.where(index == lane.astype(F32), 1.0, 0.0).astype(BF16)
        for p in range(3):
            pick_b[rows, p * K : (p + 1) * K] = hot
    fill(table)
    box = along_range()
    squares = []
    for t in range(HALF):
        parts = [acq_rows(recv_ref, part, t) for part in range(2)]
        for part, x in enumerate(parts):
            enter(table, x, t * 256 + part * 128)
        squares.append(parts[0] * parts[0] + parts[1] * parts[1])
        choose(pick_a, pick_b, table, picked, t * 256, 256)
    sums = own_rows(squares)
    up_power[:, 0:128], up_power[:, 128:256] = sums[0], sums[1]
    down_power[:, 0:128], down_power[:, 128:256] = sums[4], sums[3]
    enter_power(table, sums[2], box, HALF * 256)
    choose(pick_a, pick_b, table, picked, HALF * 256, 128)

    def rows(top):
        for f, field in enumerate(cross(picked, top, HALF)):
            x = own_rows(field)
            here = pl.ds(top + f * PAIRS, 16)
            up_ref[here, 0:128], up_ref[here, 128:256] = x[0], x[1]
            down_ref[here, 0:128], down_ref[here, 128:256] = x[4], x[3]
            store_terms(terms, top + f * PAIRS, x[2])

    for_pairs(rows)
    total[...] = dot(terms[...], box)
    lane16 = lanes_of((16, 128)) & 63

    def some(top):
        size, x0, x1, inverse = coherence_of(total, picked, top, 0, HALF * 256)
        value_ref[pl.ds(top, 16), :] = jnp.where(lane16 < STEP, size, jnp.where(lane16 < STEP + 2, x0, x1) * inverse)

    for_pairs(some)


def edge_coherence(edge_ref, sums_ref, power_ref, pick_a, pick_b, table, picked, terms, total, low):
    fill(table)
    box = along_range()
    parts = [edge_ref[part * ACQ : (part + 1) * ACQ, :] for part in range(2)]
    for part, x in enumerate(parts):
        enter(table, x, part * 128)
    choose(pick_a, pick_b, table, picked, 0, 256)
    square = parts[0] * parts[0] + parts[1] * parts[1]
    for n, x in enumerate(edge_rows(power_ref[:, 0:128], power_ref[:, 128:256], square, low)):
        enter_power(table, x, box, 256 + n * 128)
    choose(pick_a, pick_b, table, picked, 256, 256)

    def rows(top):
        for f, field in enumerate(cross(picked, top, 1)):
            here = pl.ds(top + f * PAIRS, 16)
            for n, x in enumerate(edge_rows(sums_ref[here, 0:128], sums_ref[here, 128:256], field[0], low)):
                store_terms(terms, top + (2 * n + f) * PAIRS, x)

    for_pairs(rows)
    total[...] = dot(terms[...], box)


def edge_value(value_ref, total, picked, top):
    size = coherence_of(total, picked, top, 0, 256)[0] + coherence_of(total, picked, top, 1, 384)[0]
    return value_ref[pl.ds(top, 16), :] + jnp.where((lanes_of(size.shape) & 63) < STEP, size, 0.0)


def core_kernel(core_ref, sums_ref, power_ref, pick_a, pick_b, value_ref, out_ref, table, picked, terms, total):
    edge_coherence(core_ref, sums_ref, power_ref, pick_a, pick_b, table, picked, terms, total, False)

    def some(top):
        out_ref[pl.ds(top, 16), :] = edge_value(value_ref, total, picked, top)

    for_pairs(some)


def chip_kernel(chip_ref, sums_ref, power_ref, pick_a, pick_b, value_ref, out_ref, table, picked, terms, total, ends):
    edge_coherence(chip_ref, sums_ref, power_ref, pick_a, pick_b, table, picked, terms, total, True)

    def some(top):
        for p, piece in enumerate(pieces_of(edge_value(value_ref, total, picked, top), 3)):
            ends[pl.ds(top, 16), p * 128 : (p + 1) * 128] = piece

    for_pairs(some)

    n = lax.broadcasted_iota(jnp.int32, (128, 256), 0)
    m = lax.broadcasted_iota(jnp.int32, (128, 256), 1)
    c, j, o = n & 63, m >> 7, (m >> 5) & 3
    first = jnp.where(o == 0, 20 * j, jnp.where(o == 3, 1000, STEP - 2 + 2 * o + j))
    last = first + jnp.where(o == 0, 19, 0)
    same = ((n >> 6) == ((m & 1) ^ odd_row())) & (c >= first) & (c <= last)
    spread = jnp.where(same, 1.0, 0.0).astype(BF16)
    result = dot(ends[...], jnp.concatenate([spread] * 3, axis=0))
    owner = (lanes_of((8, 128)) >> 1) & 15
    for j in range(2):
        for g in range(4):
            out = None
            for p in range(PAIR_DEV):
                top = 128 * g + 8 * p
                rows_p = result[top : top + 8, j * 128 : (j + 1) * 128]
                out = rows_p if out is None else jnp.where(owner == p, rows_p, out)
            out_ref[pl.ds(16 * g + j, 8, stride=2), :] = out


def finish_kernel(got_ref, coh_ref, re_ref, im_ref):
    turned = jnp.transpose(got_ref[...])
    coh_ref[...] = turned[0:32] * 0.01
    re_ref[...] = turned[32:64]
    im_ref[...] = turned[64:96]


def call(kernel, outs, specs, scratch=(), limit=40, out_spec=VMEM, **more):
    return pl.pallas_call(
        kernel,
        out_shape=outs,
        in_specs=specs,
        out_specs=jax.tree.map(lambda _: out_spec, outs),
        scratch_shapes=[pltpu.VMEM(*x) if isinstance(x, tuple) else x for x in scratch],
        compiler_params=pltpu.CompilerParams(vmem_limit_bytes=limit * 1024 * 1024),
        **more,
    )


def f32(*shape):
    return jax.ShapeDtypeStruct(shape, F32)


def bf16(*shape):
    return jax.ShapeDtypeStruct(shape, BF16)


EDGE_OUTS = (f32(2 * PAIRS, 256),) * 2 + (f32(ACQ, 256),) * 2
OWN_OUTS = EDGE_OUTS + (bf16(PAIRS, K), bf16(PAIRS, 3 * K), f32(PAIRS, 128))
OWN_SCRATCH = (
    ((3 * K, HALF * 256 + 128), BF16),
    ((2 * PAIRS, HALF * 256 + 128), F32),
    ((2 * PAIRS, 256), BF16),
    ((2 * PAIRS, 128), F32),
)
EDGE_SCRATCH = (
    ((3 * K, 512), BF16),
    ((2 * PAIRS, 512), F32),
    ((4 * PAIRS, 256), BF16),
    ((4 * PAIRS, 128), F32),
)
CHIP_SCRATCH = EDGE_SCRATCH + (((PAIRS, 3 * 128), BF16),)


def per_device(slc_re, slc_im, pairs):
    send = call(
        pack_kernel,
        f32(DEVS * CHUNK, 128),
        [HBM] * 3,
        (
            ((ROWS, ACQ_DEV, RG), F32),
            ((ROWS, ACQ_DEV, RG), F32),
            ((2, PAIR_DEV), jnp.int32),
            ((2 * HALF, ACQ_DEV, RG), F32),
            pltpu.SemaphoreType.DMA((3,)),
        ),
        limit=40,
        out_spec=VMEM,
    )(*[pltpu.with_memory_space_constraint(x, pltpu.HBM) for x in (jnp.transpose(slc_re, (1, 0, 2)), jnp.transpose(slc_im, (1, 0, 2)), pairs.T)])
    send = send.reshape(DEVS, CHUNK // 4, 4, 128)
    recv = lax.all_to_all(send, "acq", split_axis=0, concat_axis=0, tiled=True)
    recv = recv.reshape(DEVS * CHUNK, 128)
    chip, core = call(edges_kernel, (f32(2 * ACQ + 8, 128), f32(2 * ACQ, 128)), [VMEM])(recv)
    count = lax.axis_size("az")
    across = [(i, i + 1) for i in range(1, count - 1, 2)]
    inside = [(i, i + 1) for i in range(0, count, 2)]
    chip = lax.ppermute(chip, "az", across + [(j, i) for i, j in across])
    core = lax.ppermute(core, "az", inside + [(j, i) for i, j in inside])
    cost = [pl.CostEstimate(flops=n, bytes_accessed=n, transcendentals=0) for n in (10**3, 10**3)]
    own = call(own_kernel, OWN_OUTS, [VMEM], OWN_SCRATCH, cost_estimate=cost[0])(recv)
    up, down, up_power, down_power, pick_a, pick_b, value = own
    value = call(core_kernel, f32(PAIRS, 128), [VMEM] * 6, EDGE_SCRATCH, cost_estimate=cost[1])(
        core, down, down_power, pick_a, pick_b, value
    )
    result = call(chip_kernel, f32(2 * DEVS, 128), [VMEM] * 6, CHIP_SCRATCH)(
        chip, up, up_power, pick_a, pick_b, value
    )
    got = lax.all_to_all(result.reshape(DEVS, 2, 128), "acq", split_axis=0, concat_axis=0, tiled=True)
    outs = call(finish_kernel, (f32(32, 64),) * 3, [VMEM])(got.reshape(2 * DEVS, 128))
    return tuple(x.reshape(PAIR_DEV, 2, 64) for x in outs)


def solution(mesh):
    in_specs = (P("acq", "az", None), P("acq", "az", None), P("acq", None))
    out_specs = (P("acq", "az", None), P("acq", "az", None), P("acq", "az", None))
    return jax.shard_map(per_device, mesh=mesh, in_specs=in_specs, out_specs=out_specs, check_vma=False)
```

```python
import jax
import jax.numpy as jnp
from jax import lax
from jax.experimental import pallas as pl
from jax.experimental.pallas import tpu as pltpu
from jax.sharding import PartitionSpec as P

DEVS = 32
ACQ_DEV = 6
ACQ = DEVS * ACQ_DEV
PAIR_DEV = 16
PAIRS = DEVS * PAIR_DEV
ROWS = 10
HALF = 5
RG = 1280
STEP = 40
WIDE = STEP + 19
CHUNK = 60
K = 256
F32 = jnp.float32
BF16 = jnp.bfloat16
VMEM = pl.BlockSpec(memory_space=pltpu.VMEM)
HBM = pl.BlockSpec(memory_space=pltpu.HBM)
BIG = 3.38e38
PART = 8 * ACQ_DEV


def lanes_of(shape):
    return lax.broadcasted_iota(jnp.int32, shape, len(shape) - 1)


def odd_row():
    return lax.axis_index("az") & 1


def pack_kernel(re_hbm, im_hbm, pairs_hbm, chunks, re_ref, im_ref, pairs_ref, later, sems):
    odd = odd_row()
    copies = [
        pltpu.make_async_copy(source, target, sems.at[n])
        for n, (source, target) in enumerate(((pairs_hbm, pairs_ref), (re_hbm, re_ref), (im_hbm, im_ref)))
    ]
    for copy in copies:
        copy.start()
    lane = lanes_of((ACQ_DEV, 128))
    wide = lanes_of((PAIR_DEV, 128))
    copies[0].wait()
    acq = pairs_ref[...]
    group = (acq * 171) >> 10
    local = (acq - ACQ_DEV * group) * 8 + (group & 7)
    order = lax.broadcasted_iota(jnp.int32, (2, PAIR_DEV), 0)
    index = (local + jnp.where(order == 0, 0, (group >> 3) * PART)).astype(F32)
    square = (PAIR_DEV, PAIR_DEV)
    diagonal = lax.broadcasted_iota(jnp.int32, square, 0) == lax.broadcasted_iota(jnp.int32, square, 1)
    columns = [
        jnp.sum(jnp.where(diagonal, jnp.broadcast_to(index[w : w + 1, :], square), 0.0), axis=1, keepdims=True)
        for w in range(2)
    ]
    first, second = [jnp.broadcast_to(column, (PAIR_DEV, 128)) for column in columns]
    tiles = RG // 128
    for part, ref in enumerate((re_ref, im_ref)):
        copies[1 + part].wait()
        for r in range(HALF):
            row = r + HALF + odd * (9 - 2 * (r + HALF))
            for t in range(tiles):
                x = ref[row, :, t * 128 : (t + 1) * 128]
                later[part * HALF + r, :, t * 128 : (t + 1) * 128] = pltpu.roll(x, 64, 1)
    for d in range(DEVS):
        start = STEP * d - 10
        k = start // 128
        off = start - 128 * k
        spans = []
        for t, low, high in ((k, off, min(128, off + WIDE)), (k + 1, 0, off + WIDE - 128)):
            if low < high and 0 <= t < tiles:
                spans.append((t, False, low, high))
                shifted = [(low + 64, min(high + 64, 128)), (max(low + 64, 128) - 128, high + 64 - 128)]
                spans += [(t, True, x, y) for x, y in shifted if x < y]
        masks = [(lane >= low) & (lane < high) for _, _, low, high in spans]
        for part, ref in enumerate((re_ref, im_ref)):
            for r in range(HALF):
                row = r + odd * (9 - 2 * r)
                mixed = jnp.zeros((ACQ_DEV, 128), F32)
                for (t, shifted, _, _), mask in zip(spans, masks):
                    at = slice(t * 128, (t + 1) * 128)
                    mixed = jnp.where(mask, later[part * HALF + r, :, at] if shifted else ref[row, :, at], mixed)
                top = d * CHUNK + (part * HALF + r) * ACQ_DEV
                chunks[top : top + ACQ_DEV, :] = pltpu.roll(mixed, 128 - off, 1) if off else mixed
        head = chunks[d * CHUNK : d * CHUNK + PAIR_DEV, :]
        head = jnp.where(wide == 60, first, jnp.where(wide == 61, second, head))
        chunks[d * CHUNK : d * CHUNK + PAIR_DEV, :] = head


def acq_rows(recv_ref, part, r):
    base = (part * HALF + r) * ACQ_DEV
    return jnp.concatenate(
        [recv_ref[pl.ds(base + a + 8 * g * CHUNK, 8, stride=CHUNK), :] for g in range(4) for a in range(ACQ_DEV)],
        axis=0,
    )


def edges_kernel(recv_ref, chip_ref, core_ref):
    lane = lanes_of((ACQ, 128))
    for part in range(2):
        v0, v1, v3, v4 = [acq_rows(recv_ref, part, r) for r in (0, 1, 3, 4)]
        rows = slice(part * ACQ, (part + 1) * ACQ)
        chip_ref[rows, :] = jnp.where(lane < 64, v0, pltpu.roll(v1, 64, 1))
        core_ref[rows, :] = jnp.where(lane < 64, pltpu.roll(v3, 64, 1), v4)
    chip_ref[2 * ACQ :, :] = jnp.zeros((8, 128), F32)


def pieces_of(x, count):
    out = []
    for n in range(count):
        piece = x.astype(BF16)
        out.append(piece)
        if n + 1 < count:
            x = x - piece.astype(F32)
    return out


def clamp(x):
    return jnp.minimum(jnp.maximum(x, -BIG), BIG)


def dot(x, y):
    return jnp.dot(x, y, preferred_element_type=F32)


def fill(table):
    for p in range(3):
        table[p * K + ACQ : (p + 1) * K, :] = jnp.zeros((K - ACQ, table.shape[1]), BF16)


def enter(table, x, at):
    for p, piece in enumerate(pieces_of(clamp(x), 3)):
        table[p * K : p * K + ACQ, at : at + x.shape[1]] = piece


def along_range():
    shape = (128, 128)
    k = lax.broadcasted_iota(jnp.int32, shape, 0)
    n = lax.broadcasted_iota(jnp.int32, shape, 1)
    c = n & 63
    first = jnp.where(c < STEP, c, jnp.where(c < STEP + 4, 10 + 20 * (c & 1), -1000))
    sample = k & 63
    inside = ((k >> 6) == (n >> 6)) & (sample >= first) & (sample <= first + 19)
    box = jnp.where(inside, 1.0, 0.0).astype(BF16)
    return jnp.concatenate([box, box], axis=0)


def choose(pick_a, pick_b, table, picked, at, width, parts):
    columns = slice(at, at + width)
    picked[PAIRS:, columns] = dot(pick_b[:, : parts * K], table[: parts * K, columns])
    for g in range(4):
        few = jnp.concatenate([table[p * K + g * PART : p * K + (g + 1) * PART, columns] for p in range(3)], axis=0)
        picked[128 * g : 128 * (g + 1), columns] = dot(pick_a[128 * g : 128 * (g + 1), : 3 * PART], few)


def cross(picked, top, count):
    fields = [[], []]
    for t in range(count):
        ra = picked[pl.ds(top, 16), t * 256 : t * 256 + 128]
        ia = picked[pl.ds(top, 16), t * 256 + 128 : t * 256 + 256]
        rb = picked[pl.ds(top + PAIRS, 16), t * 256 : t * 256 + 128]
        ib = picked[pl.ds(top + PAIRS, 16), t * 256 + 128 : t * 256 + 256]
        fields[0].append(ra * rb + ia * ib)
        fields[1].append(ia * rb - ra * ib)
    return fields


def own_rows(v):
    v0, v1, v2, v3, v4 = v
    low = lanes_of(v0.shape) < 64
    next_one = pltpu.roll(jnp.where(low, v4, v0), 64, 1)
    next_two = next_one + pltpu.roll(jnp.where(low, v3, v1), 64, 1)
    v12, v34 = v1 + v2, v3 + v4
    v012, v234 = v0 + v12, v2 + v34
    return [
        v012 + jnp.where(low, 0.0, next_two),
        (v012 + v3) + jnp.where(low, 0.0, next_one),
        v012 + v34,
        (v1 + v234) + jnp.where(low, next_one, 0.0),
        v234 + jnp.where(low, next_two, 0.0),
    ]


def edge_rows(near, far, edge, low):
    inside = (lanes_of(edge.shape) < 64) == low
    return near + jnp.where(inside, edge + pltpu.roll(edge, 64, 1), 0.0), far + jnp.where(inside, edge, 0.0)


def store_terms(terms, top, x):
    for n, piece in enumerate(pieces_of(x, 2)):
        terms[pl.ds(top, 16), n * 128 : (n + 1) * 128] = piece


def enter_power(table, x, box, at):
    high, mid, low = pieces_of(x, 3)
    enter(table, dot(jnp.concatenate([high, mid], axis=1), box) + dot(low, box[:128]), at)


def coherence_of(total, picked, top, row, at):
    x0 = total[pl.ds(top + 2 * row * PAIRS, 16), :]
    x1 = total[pl.ds(top + (2 * row + 1) * PAIRS, 16), :]
    wa = picked[pl.ds(top, 16), at : at + 128]
    wb = picked[pl.ds(top + PAIRS, 16), at : at + 128]
    inverse = lax.rsqrt(wa * wb + 1e-06)
    num = x0 * x0 + x1 * x1
    return num * lax.rsqrt(jnp.maximum(num, 1e-37)) * inverse, x0, x1, inverse


def for_pairs(body):
    def step(g, carry):
        body(pl.multiple_of(16 * g, 16))
        return carry

    lax.fori_loop(0, PAIRS // 16, step, 0, unroll=True)


def own_kernel(
    recv_ref, up_ref, down_ref, up_power, down_power, pick_a, pick_b, value_ref, table, picked, terms, total
):
    lane = lanes_of((128, K))
    few = lane - PART * ((lane * 342) >> 14)
    for g in range(4):
        head = jnp.concatenate([recv_ref[pl.ds(8 * g * CHUNK + p, 8, stride=CHUNK), :] for p in range(PAIR_DEV)], axis=0)
        rows = slice(128 * g, 128 * (g + 1))
        index = jnp.broadcast_to(head[:, 60:61], (128, K))
        pick_a[rows, :] = jnp.where(index == few.astype(F32), 1.0, 0.0).astype(BF16)
        index = jnp.broadcast_to(head[:, 61:62], (128, K))
        hot = jnp.where(index == lane.astype(F32), 1.0, 0.0).astype(BF16)
        for p in range(3):
            pick_b[rows, p * K : (p + 1) * K] = hot
    fill(table)
    box = along_range()
    squares = []
    for t in range(HALF):
        parts = [acq_rows(recv_ref, part, t) for part in range(2)]
        for part, x in enumerate(parts):
            enter(table, x, t * 256 + part * 128)
        squares.append(parts[0] * parts[0] + parts[1] * parts[1])
        choose(pick_a, pick_b, table, picked, t * 256, 256, 2)
    sums = own_rows(squares)
    up_power[:, 0:128], up_power[:, 128:256] = sums[0], sums[1]
    down_power[:, 0:128], down_power[:, 128:256] = sums[4], sums[3]
    enter_power(table, sums[2], box, HALF * 256)
    choose(pick_a, pick_b, table, picked, HALF * 256, 128, 3)

    def rows(top):
        for f, field in enumerate(cross(picked, top, HALF)):
            x = own_rows(field)
            here = pl.ds(top + f * PAIRS, 16)
            up_ref[here, 0:128], up_ref[here, 128:256] = x[0], x[1]
            down_ref[here, 0:128], down_ref[here, 128:256] = x[4], x[3]
            store_terms(terms, top + f * PAIRS, x[2])

    for_pairs(rows)
    total[...] = dot(terms[...], box)
    lane16 = lanes_of((16, 128)) & 63

    def some(top):
        size, x0, x1, inverse = coherence_of(total, picked, top, 0, HALF * 256)
        value_ref[pl.ds(top, 16), :] = jnp.where(lane16 < STEP, size, jnp.where(lane16 < STEP + 2, x0, x1) * inverse)

    for_pairs(some)


def edge_coherence(edge_ref, sums_ref, power_ref, pick_a, pick_b, table, picked, terms, total, low):
    fill(table)
    box = along_range()
    parts = [edge_ref[part * ACQ : (part + 1) * ACQ, :] for part in range(2)]
    for part, x in enumerate(parts):
        enter(table, x, part * 128)
    choose(pick_a, pick_b, table, picked, 0, 256, 2)
    square = parts[0] * parts[0] + parts[1] * parts[1]
    for n, x in enumerate(edge_rows(power_ref[:, 0:128], power_ref[:, 128:256], square, low)):
        enter_power(table, x, box, 256 + n * 128)
    choose(pick_a, pick_b, table, picked, 256, 256, 3)

    def rows(top):
        for f, field in enumerate(cross(picked, top, 1)):
            here = pl.ds(top + f * PAIRS, 16)
            for n, x in enumerate(edge_rows(sums_ref[here, 0:128], sums_ref[here, 128:256], field[0], low)):
                store_terms(terms, top + (2 * n + f) * PAIRS, x)

    for_pairs(rows)
    total[...] = dot(terms[...], box)


def edge_value(value_ref, total, picked, top):
    size = coherence_of(total, picked, top, 0, 256)[0] + coherence_of(total, picked, top, 1, 384)[0]
    return value_ref[pl.ds(top, 16), :] + jnp.where((lanes_of(size.shape) & 63) < STEP, size, 0.0)


def core_kernel(core_ref, sums_ref, power_ref, pick_a, pick_b, value_ref, out_ref, table, picked, terms, total):
    edge_coherence(core_ref, sums_ref, power_ref, pick_a, pick_b, table, picked, terms, total, False)

    def some(top):
        out_ref[pl.ds(top, 16), :] = edge_value(value_ref, total, picked, top)

    for_pairs(some)


def chip_kernel(chip_ref, sums_ref, power_ref, pick_a, pick_b, value_ref, out_ref, table, picked, terms, total, ends):
    edge_coherence(chip_ref, sums_ref, power_ref, pick_a, pick_b, table, picked, terms, total, True)

    def some(top):
        for p, piece in enumerate(pieces_of(edge_value(value_ref, total, picked, top), 3)):
            ends[pl.ds(top, 16), p * 128 : (p + 1) * 128] = piece

    for_pairs(some)

    n = lax.broadcasted_iota(jnp.int32, (128, 256), 0)
    m = lax.broadcasted_iota(jnp.int32, (128, 256), 1)
    c, j, o = n & 63, m >> 7, (m >> 5) & 3
    first = jnp.where(o == 0, 20 * j, jnp.where(o == 3, 1000, STEP - 2 + 2 * o + j))
    last = first + jnp.where(o == 0, 19, 0)
    same = ((n >> 6) == ((m & 1) ^ odd_row())) & (c >= first) & (c <= last)
    spread = jnp.where(same, 1.0, 0.0).astype(BF16)
    result = dot(ends[...], jnp.concatenate([spread] * 3, axis=0))
    owner = (lanes_of((8, 128)) >> 1) & 15
    for j in range(2):
        for g in range(4):
            out = None
            for p in range(PAIR_DEV):
                top = 128 * g + 8 * p
                rows_p = result[top : top + 8, j * 128 : (j + 1) * 128]
                out = rows_p if out is None else jnp.where(owner == p, rows_p, out)
            out_ref[pl.ds(16 * g + j, 8, stride=2), :] = out


def finish_kernel(got_ref, coh_ref, re_ref, im_ref):
    turned = jnp.transpose(got_ref[...])
    coh_ref[...] = turned[0:32] * 0.01
    re_ref[...] = turned[32:64]
    im_ref[...] = turned[64:96]


def call(kernel, outs, specs, scratch=(), limit=40, out_spec=VMEM, **more):
    return pl.pallas_call(
        kernel,
        out_shape=outs,
        in_specs=specs,
        out_specs=jax.tree.map(lambda _: out_spec, outs),
        scratch_shapes=[pltpu.VMEM(*x) if isinstance(x, tuple) else x for x in scratch],
        compiler_params=pltpu.CompilerParams(vmem_limit_bytes=limit * 1024 * 1024),
        **more,
    )


def f32(*shape):
    return jax.ShapeDtypeStruct(shape, F32)


def bf16(*shape):
    return jax.ShapeDtypeStruct(shape, BF16)


EDGE_OUTS = (f32(2 * PAIRS, 256),) * 2 + (f32(ACQ, 256),) * 2
OWN_OUTS = EDGE_OUTS + (bf16(PAIRS, K), bf16(PAIRS, 3 * K), f32(PAIRS, 128))
OWN_SCRATCH = (
    ((3 * K, HALF * 256 + 128), BF16),
    ((2 * PAIRS, HALF * 256 + 128), F32),
    ((2 * PAIRS, 256), BF16),
    ((2 * PAIRS, 128), F32),
)
EDGE_SCRATCH = (
    ((3 * K, 512), BF16),
    ((2 * PAIRS, 512), F32),
    ((4 * PAIRS, 256), BF16),
    ((4 * PAIRS, 128), F32),
)
CHIP_SCRATCH = EDGE_SCRATCH + (((PAIRS, 3 * 128), BF16),)


def per_device(slc_re, slc_im, pairs):
    send = call(
        pack_kernel,
        f32(DEVS * CHUNK, 128),
        [HBM] * 3,
        (
            ((ROWS, ACQ_DEV, RG), F32),
            ((ROWS, ACQ_DEV, RG), F32),
            ((2, PAIR_DEV), jnp.int32),
            ((2 * HALF, ACQ_DEV, RG), F32),
            pltpu.SemaphoreType.DMA((3,)),
        ),
        limit=40,
        out_spec=VMEM,
    )(*[pltpu.with_memory_space_constraint(x, pltpu.HBM) for x in (jnp.transpose(slc_re, (1, 0, 2)), jnp.transpose(slc_im, (1, 0, 2)), pairs.T)])
    send = send.reshape(DEVS, CHUNK // 4, 4, 128)
    recv = lax.all_to_all(send, "acq", split_axis=0, concat_axis=0, tiled=True)
    recv = recv.reshape(DEVS * CHUNK, 128)
    chip, core = call(edges_kernel, (f32(2 * ACQ + 8, 128), f32(2 * ACQ, 128)), [VMEM])(recv)
    count = lax.axis_size("az")
    across = [(i, i + 1) for i in range(1, count - 1, 2)]
    inside = [(i, i + 1) for i in range(0, count, 2)]
    chip = lax.ppermute(chip, "az", across + [(j, i) for i, j in across])
    core = lax.ppermute(core, "az", inside + [(j, i) for i, j in inside])
    cost = [pl.CostEstimate(flops=n, bytes_accessed=n, transcendentals=0) for n in (10**3, 10**3)]
    own = call(own_kernel, OWN_OUTS, [VMEM], OWN_SCRATCH, cost_estimate=cost[0])(recv)
    up, down, up_power, down_power, pick_a, pick_b, value = own
    value = call(core_kernel, f32(PAIRS, 128), [VMEM] * 6, EDGE_SCRATCH, cost_estimate=cost[1])(
        core, down, down_power, pick_a, pick_b, value
    )
    result = call(chip_kernel, f32(2 * DEVS, 128), [VMEM] * 6, CHIP_SCRATCH)(
        chip, up, up_power, pick_a, pick_b, value
    )
    got = lax.all_to_all(result.reshape(DEVS, 2, 128), "acq", split_axis=0, concat_axis=0, tiled=True)
    outs = call(finish_kernel, (f32(32, 64),) * 3, [VMEM])(got.reshape(2 * DEVS, 128))
    return tuple(x.reshape(PAIR_DEV, 2, 64) for x in outs)


def solution(mesh):
    in_specs = (P("acq", "az", None), P("acq", "az", None), P("acq", None))
    out_specs = (P("acq", "az", None), P("acq", "az", None), P("acq", "az", None))
    return jax.shard_map(per_device, mesh=mesh, in_specs=in_specs, out_specs=out_specs, check_vma=False)
```

```python
import jax
import jax.numpy as jnp
from jax import lax
from jax.experimental import pallas as pl
from jax.experimental.pallas import tpu as pltpu
from jax.sharding import PartitionSpec as P

DEVS = 32
ACQ_DEV = 6
ACQ = DEVS * ACQ_DEV
PAIR_DEV = 16
PAIRS = DEVS * PAIR_DEV
ROWS = 10
HALF = 5
RG = 1280
STEP = 40
WIDE = STEP + 19
CHUNK = 60
K = 256
F32 = jnp.float32
BF16 = jnp.bfloat16
VMEM = pl.BlockSpec(memory_space=pltpu.VMEM)
HBM = pl.BlockSpec(memory_space=pltpu.HBM)
BIG = 3.38e38
PART = 8 * ACQ_DEV


def lanes_of(shape):
    return lax.broadcasted_iota(jnp.int32, shape, len(shape) - 1)


def odd_row():
    return lax.axis_index("az") & 1


def pack_kernel(re_hbm, im_hbm, pairs_hbm, chunks, re_ref, im_ref, pairs_ref, later, sems):
    odd = odd_row()
    copies = [
        pltpu.make_async_copy(source, target, sems.at[n])
        for n, (source, target) in enumerate(((pairs_hbm, pairs_ref), (re_hbm, re_ref), (im_hbm, im_ref)))
    ]
    for copy in copies:
        copy.start()
    lane = lanes_of((ACQ_DEV, 128))
    wide = lanes_of((PAIR_DEV, 128))
    copies[0].wait()
    acq = pairs_ref[...]
    group = (acq * 171) >> 10
    local = (acq - ACQ_DEV * group) * 8 + (group & 7)
    order = lax.broadcasted_iota(jnp.int32, (2, PAIR_DEV), 0)
    index = (local + jnp.where(order == 0, 0, (group >> 3) * PART)).astype(F32)
    square = (PAIR_DEV, PAIR_DEV)
    diagonal = lax.broadcasted_iota(jnp.int32, square, 0) == lax.broadcasted_iota(jnp.int32, square, 1)
    columns = [
        jnp.sum(jnp.where(diagonal, jnp.broadcast_to(index[w : w + 1, :], square), 0.0), axis=1, keepdims=True)
        for w in range(2)
    ]
    first, second = [jnp.broadcast_to(column, (PAIR_DEV, 128)) for column in columns]
    tiles = RG // 128
    for part, ref in enumerate((re_ref, im_ref)):
        copies[1 + part].wait()
        for r in range(HALF):
            row = r + HALF + odd * (9 - 2 * (r + HALF))
            for t in range(tiles):
                x = ref[row, :, t * 128 : (t + 1) * 128]
                later[part * HALF + r, :, t * 128 : (t + 1) * 128] = pltpu.roll(x, 64, 1)
    for d in range(DEVS):
        start = STEP * d - 10
        k = start // 128
        off = start - 128 * k
        spans = []
        for t, low, high in ((k, off, min(128, off + WIDE)), (k + 1, 0, off + WIDE - 128)):
            if low < high and 0 <= t < tiles:
                spans.append((t, False, low, high))
                shifted = [(low + 64, min(high + 64, 128)), (max(low + 64, 128) - 128, high + 64 - 128)]
                spans += [(t, True, x, y) for x, y in shifted if x < y]
        masks = [(lane >= low) & (lane < high) for _, _, low, high in spans]
        for part, ref in enumerate((re_ref, im_ref)):
            for r in range(HALF):
                row = r + odd * (9 - 2 * r)
                mixed = jnp.zeros((ACQ_DEV, 128), F32)
                for (t, shifted, _, _), mask in zip(spans, masks):
                    at = slice(t * 128, (t + 1) * 128)
                    mixed = jnp.where(mask, later[part * HALF + r, :, at] if shifted else ref[row, :, at], mixed)
                top = d * CHUNK + (part * HALF + r) * ACQ_DEV
                chunks[top : top + ACQ_DEV, :] = pltpu.roll(mixed, 128 - off, 1) if off else mixed
        head = chunks[d * CHUNK : d * CHUNK + PAIR_DEV, :]
        head = jnp.where(wide == 60, first, jnp.where(wide == 61, second, head))
        chunks[d * CHUNK : d * CHUNK + PAIR_DEV, :] = head


def acq_rows(recv_ref, part, r):
    base = (part * HALF + r) * ACQ_DEV
    return jnp.concatenate(
        [recv_ref[pl.ds(base + a + 8 * g * CHUNK, 8, stride=CHUNK), :] for g in range(4) for a in range(ACQ_DEV)],
        axis=0,
    )


def edges_kernel(recv_ref, chip_ref, core_ref):
    lane = lanes_of((ACQ, 128))
    for part in range(2):
        v0, v1, v3, v4 = [acq_rows(recv_ref, part, r) for r in (0, 1, 3, 4)]
        rows = slice(part * ACQ, (part + 1) * ACQ)
        chip_ref[rows, :] = jnp.where(lane < 64, v0, pltpu.roll(v1, 64, 1))
        core_ref[rows, :] = jnp.where(lane < 64, pltpu.roll(v3, 64, 1), v4)
    chip_ref[2 * ACQ :, :] = jnp.zeros((8, 128), F32)


def pieces_of(x, count):
    out = []
    for n in range(count):
        piece = x.astype(BF16)
        out.append(piece)
        if n + 1 < count:
            x = x - piece.astype(F32)
    return out


def clamp(x):
    return jnp.minimum(jnp.maximum(x, -BIG), BIG)


def dot(x, y):
    return jnp.dot(x, y, preferred_element_type=F32)


def fill(table):
    for p in range(3):
        table[p * K + ACQ : (p + 1) * K, :] = jnp.zeros((K - ACQ, table.shape[1]), BF16)


def enter(table, x, at):
    for p, piece in enumerate(pieces_of(clamp(x), 3)):
        table[p * K : p * K + ACQ, at : at + x.shape[1]] = piece


def along_range():
    shape = (128, 128)
    k = lax.broadcasted_iota(jnp.int32, shape, 0)
    n = lax.broadcasted_iota(jnp.int32, shape, 1)
    c = n & 63
    first = jnp.where(c < STEP, c, jnp.where(c < STEP + 4, 10 + 20 * (c & 1), -1000))
    sample = k & 63
    inside = ((k >> 6) == (n >> 6)) & (sample >= first) & (sample <= first + 19)
    box = jnp.where(inside, 1.0, 0.0).astype(BF16)
    return jnp.concatenate([box, box], axis=0)


def choose(pick_a, pick_b, table, picked, at, width, parts):
    columns = slice(at, at + width)
    picked[PAIRS:, columns] = dot(pick_b[:, : parts * K], table[: parts * K, columns])
    for g in range(4):
        few = jnp.concatenate([table[p * K + g * PART : p * K + (g + 1) * PART, columns] for p in range(3)], axis=0)
        picked[128 * g : 128 * (g + 1), columns] = dot(pick_a[128 * g : 128 * (g + 1), : 3 * PART], few)


def cross(picked, top, count):
    fields = [[], []]
    for t in range(count):
        ra = picked[pl.ds(top, 16), t * 256 : t * 256 + 128]
        ia = picked[pl.ds(top, 16), t * 256 + 128 : t * 256 + 256]
        rb = picked[pl.ds(top + PAIRS, 16), t * 256 : t * 256 + 128]
        ib = picked[pl.ds(top + PAIRS, 16), t * 256 + 128 : t * 256 + 256]
        fields[0].append(ra * rb + ia * ib)
        fields[1].append(ia * rb - ra * ib)
    return fields


def own_rows(v):
    v0, v1, v2, v3, v4 = v
    low = lanes_of(v0.shape) < 64
    next_one = pltpu.roll(jnp.where(low, v4, v0), 64, 1)
    next_two = next_one + pltpu.roll(jnp.where(low, v3, v1), 64, 1)
    v12, v34 = v1 + v2, v3 + v4
    v012, v234 = v0 + v12, v2 + v34
    return [
        v012 + jnp.where(low, 0.0, next_two),
        (v012 + v3) + jnp.where(low, 0.0, next_one),
        v012 + v34,
        (v1 + v234) + jnp.where(low, next_one, 0.0),
        v234 + jnp.where(low, next_two, 0.0),
    ]


def edge_rows(near, far, edge, low):
    inside = (lanes_of(edge.shape) < 64) == low
    return near + jnp.where(inside, edge + pltpu.roll(edge, 64, 1), 0.0), far + jnp.where(inside, edge, 0.0)


def store_terms(terms, top, x):
    for n, piece in enumerate(pieces_of(x, 2)):
        terms[pl.ds(top, 16), n * 128 : (n + 1) * 128] = piece


def enter_power(table, x, box, at):
    high, mid, low = pieces_of(x, 3)
    enter(table, dot(jnp.concatenate([high, mid], axis=1), box) + dot(low, box[:128]), at)


def coherence_of(total, picked, top, row, at):
    x0 = total[pl.ds(top + 2 * row * PAIRS, 16), :]
    x1 = total[pl.ds(top + (2 * row + 1) * PAIRS, 16), :]
    wa = picked[pl.ds(top, 16), at : at + 128]
    wb = picked[pl.ds(top + PAIRS, 16), at : at + 128]
    inverse = lax.rsqrt(wa * wb + 1e-06)
    num = x0 * x0 + x1 * x1
    return num * lax.rsqrt(jnp.maximum(num, 1e-37)) * inverse, x0, x1, inverse


def for_pairs(body):
    def step(g, carry):
        body(pl.multiple_of(16 * g, 16))
        return carry

    lax.fori_loop(0, PAIRS // 16, step, 0, unroll=True)


def own_kernel(
    recv_ref, up_ref, down_ref, up_power, down_power, pick_a, pick_b, value_ref, table, picked, terms, total
):
    lane = lanes_of((128, K))
    few = lane - PART * ((lane * 342) >> 14)
    for g in range(4):
        head = jnp.concatenate([recv_ref[pl.ds(8 * g * CHUNK + p, 8, stride=CHUNK), :] for p in range(PAIR_DEV)], axis=0)
        rows = slice(128 * g, 128 * (g + 1))
        index = jnp.broadcast_to(head[:, 60:61], (128, K))
        pick_a[rows, :] = jnp.where(index == few.astype(F32), 1.0, 0.0).astype(BF16)
        index = jnp.broadcast_to(head[:, 61:62], (128, K))
        hot = jnp.where(index == lane.astype(F32), 1.0, 0.0).astype(BF16)
        for p in range(3):
            pick_b[rows, p * K : (p + 1) * K] = hot
    fill(table)
    box = along_range()
    squares = []
    for t in range(HALF):
        parts = [acq_rows(recv_ref, part, t) for part in range(2)]
        for part, x in enumerate(parts):
            enter(table, x, t * 256 + part * 128)
        squares.append(parts[0] * parts[0] + parts[1] * parts[1])
        choose(pick_a, pick_b, table, picked, t * 256, 256, 2)
    sums = own_rows(squares)
    up_power[:, 0:128], up_power[:, 128:256] = sums[0], sums[1]
    down_power[:, 0:128], down_power[:, 128:256] = sums[4], sums[3]
    enter_power(table, sums[2], box, HALF * 256)
    choose(pick_a, pick_b, table, picked, HALF * 256, 128, 3)

    def rows(top):
        for f, field in enumerate(cross(picked, top, HALF)):
            x = own_rows(field)
            here = pl.ds(top + f * PAIRS, 16)
            up_ref[here, 0:128], up_ref[here, 128:256] = x[0], x[1]
            down_ref[here, 0:128], down_ref[here, 128:256] = x[4], x[3]
            store_terms(terms, top + f * PAIRS, x[2])

    for_pairs(rows)
    total[...] = dot(terms[...], box)
    lane16 = lanes_of((16, 128)) & 63

    def some(top):
        size, x0, x1, inverse = coherence_of(total, picked, top, 0, HALF * 256)
        value_ref[pl.ds(top, 16), :] = jnp.where(lane16 < STEP, size, jnp.where(lane16 < STEP + 2, x0, x1) * inverse)

    for_pairs(some)


def edge_coherence(edge_ref, sums_ref, power_ref, pick_a, pick_b, table, picked, terms, total, low):
    fill(table)
    box = along_range()
    parts = [edge_ref[part * ACQ : (part + 1) * ACQ, :] for part in range(2)]
    for part, x in enumerate(parts):
        enter(table, x, part * 128)
    square = parts[0] * parts[0] + parts[1] * parts[1]
    for n, x in enumerate(edge_rows(power_ref[:, 0:128], power_ref[:, 128:256], square, low)):
        enter_power(table, x, box, 256 + n * 128)
    choose(pick_a, pick_b, table, picked, 0, 256, 2)
    choose(pick_a, pick_b, table, picked, 256, 256, 3)

    def rows(top):
        for f, field in enumerate(cross(picked, top, 1)):
            here = pl.ds(top + f * PAIRS, 16)
            for n, x in enumerate(edge_rows(sums_ref[here, 0:128], sums_ref[here, 128:256], field[0], low)):
                store_terms(terms, top + (2 * n + f) * PAIRS, x)

    for_pairs(rows)
    total[...] = dot(terms[...], box)


def edge_value(value_ref, total, picked, top):
    size = coherence_of(total, picked, top, 0, 256)[0] + coherence_of(total, picked, top, 1, 384)[0]
    return value_ref[pl.ds(top, 16), :] + jnp.where((lanes_of(size.shape) & 63) < STEP, size, 0.0)


def core_kernel(core_ref, sums_ref, power_ref, pick_a, pick_b, value_ref, out_ref, table, picked, terms, total):
    edge_coherence(core_ref, sums_ref, power_ref, pick_a, pick_b, table, picked, terms, total, False)

    def some(top):
        out_ref[pl.ds(top, 16), :] = edge_value(value_ref, total, picked, top)

    for_pairs(some)


def chip_kernel(chip_ref, sums_ref, power_ref, pick_a, pick_b, value_ref, out_ref, table, picked, terms, total, ends):
    edge_coherence(chip_ref, sums_ref, power_ref, pick_a, pick_b, table, picked, terms, total, True)

    def some(top):
        for p, piece in enumerate(pieces_of(edge_value(value_ref, total, picked, top), 3)):
            ends[pl.ds(top, 16), p * 128 : (p + 1) * 128] = piece

    for_pairs(some)

    n = lax.broadcasted_iota(jnp.int32, (128, 256), 0)
    m = lax.broadcasted_iota(jnp.int32, (128, 256), 1)
    c, j, o = n & 63, m >> 7, (m >> 5) & 3
    first = jnp.where(o == 0, 20 * j, jnp.where(o == 3, 1000, STEP - 2 + 2 * o + j))
    last = first + jnp.where(o == 0, 19, 0)
    same = ((n >> 6) == ((m & 1) ^ odd_row())) & (c >= first) & (c <= last)
    spread = jnp.where(same, 1.0, 0.0).astype(BF16)
    result = dot(ends[...], jnp.concatenate([spread] * 3, axis=0))
    owner = (lanes_of((8, 128)) >> 1) & 15
    for j in range(2):
        for g in range(4):
            out = None
            for p in range(PAIR_DEV):
                top = 128 * g + 8 * p
                rows_p = result[top : top + 8, j * 128 : (j + 1) * 128]
                out = rows_p if out is None else jnp.where(owner == p, rows_p, out)
            out_ref[pl.ds(16 * g + j, 8, stride=2), :] = out


def finish_kernel(got_ref, coh_ref, re_ref, im_ref):
    turned = jnp.transpose(got_ref[...])
    coh_ref[...] = turned[0:32] * 0.01
    re_ref[...] = turned[32:64]
    im_ref[...] = turned[64:96]


def call(kernel, outs, specs, scratch=(), limit=40, out_spec=VMEM, **more):
    return pl.pallas_call(
        kernel,
        out_shape=outs,
        in_specs=specs,
        out_specs=jax.tree.map(lambda _: out_spec, outs),
        scratch_shapes=[pltpu.VMEM(*x) if isinstance(x, tuple) else x for x in scratch],
        compiler_params=pltpu.CompilerParams(vmem_limit_bytes=limit * 1024 * 1024),
        **more,
    )


def f32(*shape):
    return jax.ShapeDtypeStruct(shape, F32)


def bf16(*shape):
    return jax.ShapeDtypeStruct(shape, BF16)


EDGE_OUTS = (f32(2 * PAIRS, 256),) * 2 + (f32(ACQ, 256),) * 2
OWN_OUTS = EDGE_OUTS + (bf16(PAIRS, K), bf16(PAIRS, 3 * K), f32(PAIRS, 128))
OWN_SCRATCH = (
    ((3 * K, HALF * 256 + 128), BF16),
    ((2 * PAIRS, HALF * 256 + 128), F32),
    ((2 * PAIRS, 256), BF16),
    ((2 * PAIRS, 128), F32),
)
EDGE_SCRATCH = (
    ((3 * K, 512), BF16),
    ((2 * PAIRS, 512), F32),
    ((4 * PAIRS, 256), BF16),
    ((4 * PAIRS, 128), F32),
)
CHIP_SCRATCH = EDGE_SCRATCH + (((PAIRS, 3 * 128), BF16),)


def per_device(slc_re, slc_im, pairs):
    send = call(
        pack_kernel,
        f32(DEVS * CHUNK, 128),
        [HBM] * 3,
        (
            ((ROWS, ACQ_DEV, RG), F32),
            ((ROWS, ACQ_DEV, RG), F32),
            ((2, PAIR_DEV), jnp.int32),
            ((2 * HALF, ACQ_DEV, RG), F32),
            pltpu.SemaphoreType.DMA((3,)),
        ),
        limit=40,
        out_spec=VMEM,
    )(*[pltpu.with_memory_space_constraint(x, pltpu.HBM) for x in (jnp.transpose(slc_re, (1, 0, 2)), jnp.transpose(slc_im, (1, 0, 2)), pairs.T)])
    send = send.reshape(DEVS, CHUNK // 4, 4, 128)
    recv = lax.all_to_all(send, "acq", split_axis=0, concat_axis=0, tiled=True)
    recv = recv.reshape(DEVS * CHUNK, 128)
    chip, core = call(edges_kernel, (f32(2 * ACQ + 8, 128), f32(2 * ACQ, 128)), [VMEM])(recv)
    count = lax.axis_size("az")
    across = [(i, i + 1) for i in range(1, count - 1, 2)]
    inside = [(i, i + 1) for i in range(0, count, 2)]
    chip = lax.ppermute(chip, "az", across + [(j, i) for i, j in across])
    core = lax.ppermute(core, "az", inside + [(j, i) for i, j in inside])
    cost = [pl.CostEstimate(flops=n, bytes_accessed=n, transcendentals=0) for n in (10**3, 10**3)]
    own = call(own_kernel, OWN_OUTS, [VMEM], OWN_SCRATCH, cost_estimate=cost[0])(recv)
    up, down, up_power, down_power, pick_a, pick_b, value = own
    value = call(core_kernel, f32(PAIRS, 128), [VMEM] * 6, EDGE_SCRATCH, cost_estimate=cost[1])(
        core, down, down_power, pick_a, pick_b, value
    )
    result = call(chip_kernel, f32(2 * DEVS, 128), [VMEM] * 6, CHIP_SCRATCH)(
        chip, up, up_power, pick_a, pick_b, value
    )
    got = lax.all_to_all(result.reshape(DEVS, 2, 128), "acq", split_axis=0, concat_axis=0, tiled=True)
    outs = call(finish_kernel, (f32(32, 64),) * 3, [VMEM])(got.reshape(2 * DEVS, 128))
    return tuple(x.reshape(PAIR_DEV, 2, 64) for x in outs)


def solution(mesh):
    in_specs = (P("acq", "az", None), P("acq", "az", None), P("acq", None))
    out_specs = (P("acq", "az", None), P("acq", "az", None), P("acq", "az", None))
    return jax.shard_map(per_device, mesh=mesh, in_specs=in_specs, out_specs=out_specs, check_vma=False)
```

```python
import jax
import jax.numpy as jnp
from jax import lax
from jax.experimental import pallas as pl
from jax.experimental.pallas import tpu as pltpu
from jax.sharding import PartitionSpec as P

DEVS = 32
ACQ_DEV = 6
ACQ = DEVS * ACQ_DEV
PAIR_DEV = 16
PAIRS = DEVS * PAIR_DEV
ROWS = 10
HALF = 5
RG = 1280
STEP = 40
WIDE = STEP + 19
CHUNK = 60
K = 256
F32 = jnp.float32
BF16 = jnp.bfloat16
VMEM = pl.BlockSpec(memory_space=pltpu.VMEM)
HBM = pl.BlockSpec(memory_space=pltpu.HBM)
BIG = 3.38e38
PART = 8 * ACQ_DEV


def lanes_of(shape):
    return lax.broadcasted_iota(jnp.int32, shape, len(shape) - 1)


def odd_row():
    return lax.axis_index("az") & 1


def pack_kernel(re_hbm, im_hbm, pairs_hbm, chunks, re_ref, im_ref, pairs_ref, later, sems):
    odd = odd_row()
    copies = [
        pltpu.make_async_copy(source, target, sems.at[n])
        for n, (source, target) in enumerate(((pairs_hbm, pairs_ref), (re_hbm, re_ref), (im_hbm, im_ref)))
    ]
    for copy in copies:
        copy.start()
    lane = lanes_of((ACQ_DEV, 128))
    wide = lanes_of((PAIR_DEV, 128))
    copies[0].wait()
    acq = pairs_ref[...]
    group = (acq * 171) >> 10
    local = (acq - ACQ_DEV * group) * 8 + (group & 7)
    order = lax.broadcasted_iota(jnp.int32, (2, PAIR_DEV), 0)
    index = (local + jnp.where(order == 0, 0, (group >> 3) * PART)).astype(F32)
    square = (PAIR_DEV, PAIR_DEV)
    diagonal = lax.broadcasted_iota(jnp.int32, square, 0) == lax.broadcasted_iota(jnp.int32, square, 1)
    columns = [
        jnp.sum(jnp.where(diagonal, jnp.broadcast_to(index[w : w + 1, :], square), 0.0), axis=1, keepdims=True)
        for w in range(2)
    ]
    first, second = [jnp.broadcast_to(column, (PAIR_DEV, 128)) for column in columns]
    tiles = RG // 128
    for part, ref in enumerate((re_ref, im_ref)):
        copies[1 + part].wait()
        for r in range(HALF):
            row = r + HALF + odd * (9 - 2 * (r + HALF))
            for t in range(tiles):
                x = ref[row, :, t * 128 : (t + 1) * 128]
                later[part * HALF + r, :, t * 128 : (t + 1) * 128] = pltpu.roll(x, 64, 1)
    for d in range(DEVS):
        start = STEP * d - 10
        k = start // 128
        off = start - 128 * k
        spans = []
        for t, low, high in ((k, off, min(128, off + WIDE)), (k + 1, 0, off + WIDE - 128)):
            if low < high and 0 <= t < tiles:
                spans.append((t, False, low, high))
                shifted = [(low + 64, min(high + 64, 128)), (max(low + 64, 128) - 128, high + 64 - 128)]
                spans += [(t, True, x, y) for x, y in shifted if x < y]
        masks = [(lane >= low) & (lane < high) for _, _, low, high in spans]
        for part, ref in enumerate((re_ref, im_ref)):
            for r in range(HALF):
                row = r + odd * (9 - 2 * r)
                mixed = jnp.zeros((ACQ_DEV, 128), F32)
                for (t, shifted, _, _), mask in zip(spans, masks):
                    at = slice(t * 128, (t + 1) * 128)
                    mixed = jnp.where(mask, later[part * HALF + r, :, at] if shifted else ref[row, :, at], mixed)
                top = d * CHUNK + (part * HALF + r) * ACQ_DEV
                chunks[top : top + ACQ_DEV, :] = pltpu.roll(mixed, 128 - off, 1) if off else mixed
        head = chunks[d * CHUNK : d * CHUNK + PAIR_DEV, :]
        head = jnp.where(wide == 60, first, jnp.where(wide == 61, second, head))
        chunks[d * CHUNK : d * CHUNK + PAIR_DEV, :] = head


def acq_rows(recv_ref, part, r):
    base = (part * HALF + r) * ACQ_DEV
    return jnp.concatenate(
        [recv_ref[pl.ds(base + a + 8 * g * CHUNK, 8, stride=CHUNK), :] for g in range(4) for a in range(ACQ_DEV)],
        axis=0,
    )


def edges_kernel(recv_ref, chip_ref, core_ref):
    lane = lanes_of((ACQ, 128))
    for part in range(2):
        v0, v1, v3, v4 = [acq_rows(recv_ref, part, r) for r in (0, 1, 3, 4)]
        rows = slice(part * ACQ, (part + 1) * ACQ)
        chip_ref[rows, :] = jnp.where(lane < 64, v0, pltpu.roll(v1, 64, 1))
        core_ref[rows, :] = jnp.where(lane < 64, pltpu.roll(v3, 64, 1), v4)
    chip_ref[2 * ACQ :, :] = jnp.zeros((8, 128), F32)


def pieces_of(x, count):
    out = []
    for n in range(count):
        piece = x.astype(BF16)
        out.append(piece)
        if n + 1 < count:
            x = x - piece.astype(F32)
    return out


def clamp(x):
    return jnp.minimum(jnp.maximum(x, -BIG), BIG)


def dot(x, y):
    return jnp.dot(x, y, preferred_element_type=F32)


def fill(table):
    for p in range(3):
        table[p * K + ACQ : (p + 1) * K, :] = jnp.zeros((K - ACQ, table.shape[1]), BF16)


def enter(table, x, at):
    for p, piece in enumerate(pieces_of(clamp(x), 3)):
        table[p * K : p * K + ACQ, at : at + x.shape[1]] = piece


def along_range():
    shape = (128, 128)
    k = lax.broadcasted_iota(jnp.int32, shape, 0)
    n = lax.broadcasted_iota(jnp.int32, shape, 1)
    c = n & 63
    first = jnp.where(c < STEP, c, jnp.where(c < STEP + 4, 10 + 20 * (c & 1), -1000))
    sample = k & 63
    inside = ((k >> 6) == (n >> 6)) & (sample >= first) & (sample <= first + 19)
    box = jnp.where(inside, 1.0, 0.0).astype(BF16)
    return jnp.concatenate([box, box], axis=0)


def choose(pick_a, pick_b, table, picked, at, width, parts):
    columns = slice(at, at + width)
    picked[PAIRS:, columns] = dot(pick_b[:, : parts * K], table[: parts * K, columns])
    for g in range(4):
        few = jnp.concatenate([table[p * K + g * PART : p * K + (g + 1) * PART, columns] for p in range(3)], axis=0)
        picked[128 * g : 128 * (g + 1), columns] = dot(pick_a[128 * g : 128 * (g + 1), : 3 * PART], few)


def cross(picked, top, count):
    fields = [[], []]
    for t in range(count):
        ra = picked[pl.ds(top, 16), t * 256 : t * 256 + 128]
        ia = picked[pl.ds(top, 16), t * 256 + 128 : t * 256 + 256]
        rb = picked[pl.ds(top + PAIRS, 16), t * 256 : t * 256 + 128]
        ib = picked[pl.ds(top + PAIRS, 16), t * 256 + 128 : t * 256 + 256]
        fields[0].append(ra * rb + ia * ib)
        fields[1].append(ia * rb - ra * ib)
    return fields


def own_rows(v):
    v0, v1, v2, v3, v4 = v
    low = lanes_of(v0.shape) < 64
    next_one = pltpu.roll(jnp.where(low, v4, v0), 64, 1)
    next_two = next_one + pltpu.roll(jnp.where(low, v3, v1), 64, 1)
    v12, v34 = v1 + v2, v3 + v4
    v012, v234 = v0 + v12, v2 + v34
    return v012, v012 + v3, v012 + v34, v1 + v234, v234, next_two, next_one


def edge_rows(sums, turned, here, edge, low):
    inside = (lanes_of(edge.shape) < 64) == low
    two = edge + pltpu.roll(edge, 64, 1)
    near = sums[here, 0:128] + jnp.where(inside, two, turned[here, 0:128])
    return near, sums[here, 128:256] + jnp.where(inside, edge, turned[here, 128:256])


def store_terms(terms, top, x):
    for n, piece in enumerate(pieces_of(x, 2)):
        terms[pl.ds(top, 16), n * 128 : (n + 1) * 128] = piece


def enter_power(table, x, box, at):
    high, mid, low = pieces_of(x, 3)
    enter(table, dot(jnp.concatenate([high, mid], axis=1), box) + dot(low, box[:128]), at)


def coherence_of(total, picked, top, row, at):
    x0 = total[pl.ds(top + 2 * row * PAIRS, 16), :]
    x1 = total[pl.ds(top + (2 * row + 1) * PAIRS, 16), :]
    wa = picked[pl.ds(top, 16), at : at + 128]
    wb = picked[pl.ds(top + PAIRS, 16), at : at + 128]
    inverse = lax.rsqrt(wa * wb + 1e-06)
    num = x0 * x0 + x1 * x1
    return num * lax.rsqrt(jnp.maximum(num, 1e-37)) * inverse, x0, x1, inverse


def for_pairs(body):
    def step(g, carry):
        body(pl.multiple_of(16 * g, 16))
        return carry

    lax.fori_loop(0, PAIRS // 16, step, 0, unroll=True)


def own_kernel(
    recv_ref, up_ref, down_ref, turn_ref, up_power, down_power, turn_power, pick_a, pick_b, value_ref, table, picked, terms, total
):
    lane = lanes_of((128, K))
    few = lane - PART * ((lane * 342) >> 14)
    for g in range(4):
        head = jnp.concatenate([recv_ref[pl.ds(8 * g * CHUNK + p, 8, stride=CHUNK), :] for p in range(PAIR_DEV)], axis=0)
        rows = slice(128 * g, 128 * (g + 1))
        index = jnp.broadcast_to(head[:, 60:61], (128, K))
        pick_a[rows, :] = jnp.where(index == few.astype(F32), 1.0, 0.0).astype(BF16)
        index = jnp.broadcast_to(head[:, 61:62], (128, K))
        hot = jnp.where(index == lane.astype(F32), 1.0, 0.0).astype(BF16)
        for p in range(3):
            pick_b[rows, p * K : (p + 1) * K] = hot
    fill(table)
    box = along_range()
    squares = []
    for t in range(HALF):
        parts = [acq_rows(recv_ref, part, t) for part in range(2)]
        for part, x in enumerate(parts):
            enter(table, x, t * 256 + part * 128)
        squares.append(parts[0] * parts[0] + parts[1] * parts[1])
        choose(pick_a, pick_b, table, picked, t * 256, 256, 2)
    sums = own_rows(squares)
    up_power[:, 0:128], up_power[:, 128:256] = sums[0], sums[1]
    down_power[:, 0:128], down_power[:, 128:256] = sums[4], sums[3]
    turn_power[:, 0:128], turn_power[:, 128:256] = sums[5], sums[6]
    enter_power(table, sums[2], box, HALF * 256)
    choose(pick_a, pick_b, table, picked, HALF * 256, 128, 3)

    def rows(top):
        for f, field in enumerate(cross(picked, top, HALF)):
            x = own_rows(field)
            here = pl.ds(top + f * PAIRS, 16)
            up_ref[here, 0:128], up_ref[here, 128:256] = x[0], x[1]
            down_ref[here, 0:128], down_ref[here, 128:256] = x[4], x[3]
            turn_ref[here, 0:128], turn_ref[here, 128:256] = x[5], x[6]
            store_terms(terms, top + f * PAIRS, x[2])

    for_pairs(rows)
    total[...] = dot(terms[...], box)
    lane16 = lanes_of((16, 128)) & 63

    def some(top):
        size, x0, x1, inverse = coherence_of(total, picked, top, 0, HALF * 256)
        value_ref[pl.ds(top, 16), :] = jnp.where(lane16 < STEP, size, jnp.where(lane16 < STEP + 2, x0, x1) * inverse)

    for_pairs(some)


def edge_coherence(edge_ref, sums, powers, pick_a, pick_b, table, picked, terms, total, low):
    fill(table)
    box = along_range()
    parts = [edge_ref[part * ACQ : (part + 1) * ACQ, :] for part in range(2)]
    for part, x in enumerate(parts):
        enter(table, x, part * 128)
    square = parts[0] * parts[0] + parts[1] * parts[1]
    for n, x in enumerate(edge_rows(*powers, slice(0, ACQ), square, low)):
        enter_power(table, x, box, 256 + n * 128)
    choose(pick_a, pick_b, table, picked, 0, 256, 2)
    choose(pick_a, pick_b, table, picked, 256, 256, 3)

    def rows(top):
        for f, field in enumerate(cross(picked, top, 1)):
            here = pl.ds(top + f * PAIRS, 16)
            for n, x in enumerate(edge_rows(*sums, here, field[0], low)):
                store_terms(terms, top + (2 * n + f) * PAIRS, x)

    for_pairs(rows)
    total[...] = dot(terms[...], box)


def edge_value(value_ref, total, picked, top):
    size = coherence_of(total, picked, top, 0, 256)[0] + coherence_of(total, picked, top, 1, 384)[0]
    return value_ref[pl.ds(top, 16), :] + jnp.where((lanes_of(size.shape) & 63) < STEP, size, 0.0)


def core_kernel(core_ref, sums_ref, turn_ref, power_ref, turn_power, pick_a, pick_b, value_ref, out_ref, table, picked, terms, total):
    sums, powers = (sums_ref, turn_ref), (power_ref, turn_power)
    edge_coherence(core_ref, sums, powers, pick_a, pick_b, table, picked, terms, total, False)

    def some(top):
        out_ref[pl.ds(top, 16), :] = edge_value(value_ref, total, picked, top)

    for_pairs(some)


def chip_kernel(chip_ref, sums_ref, turn_ref, power_ref, turn_power, pick_a, pick_b, value_ref, out_ref, table, picked, terms, total, ends):
    sums, powers = (sums_ref, turn_ref), (power_ref, turn_power)
    edge_coherence(chip_ref, sums, powers, pick_a, pick_b, table, picked, terms, total, True)

    def some(top):
        for p, piece in enumerate(pieces_of(edge_value(value_ref, total, picked, top), 3)):
            ends[pl.ds(top, 16), p * 128 : (p + 1) * 128] = piece

    for_pairs(some)

    n = lax.broadcasted_iota(jnp.int32, (128, 256), 0)
    m = lax.broadcasted_iota(jnp.int32, (128, 256), 1)
    c, j, o = n & 63, m >> 7, (m >> 5) & 3
    first = jnp.where(o == 0, 20 * j, jnp.where(o == 3, 1000, STEP - 2 + 2 * o + j))
    last = first + jnp.where(o == 0, 19, 0)
    same = ((n >> 6) == ((m & 1) ^ odd_row())) & (c >= first) & (c <= last)
    spread = jnp.where(same, 1.0, 0.0).astype(BF16)
    result = dot(ends[...], jnp.concatenate([spread] * 3, axis=0))
    owner = (lanes_of((8, 128)) >> 1) & 15
    for j in range(2):
        for g in range(4):
            out = None
            for p in range(PAIR_DEV):
                top = 128 * g + 8 * p
                rows_p = result[top : top + 8, j * 128 : (j + 1) * 128]
                out = rows_p if out is None else jnp.where(owner == p, rows_p, out)
            out_ref[pl.ds(16 * g + j, 8, stride=2), :] = out


def finish_kernel(got_ref, coh_ref, re_ref, im_ref):
    turned = jnp.transpose(got_ref[...])
    coh_ref[...] = turned[0:32] * 0.01
    re_ref[...] = turned[32:64]
    im_ref[...] = turned[64:96]


def call(kernel, outs, specs, scratch=(), limit=40, out_spec=VMEM, **more):
    return pl.pallas_call(
        kernel,
        out_shape=outs,
        in_specs=specs,
        out_specs=jax.tree.map(lambda _: out_spec, outs),
        scratch_shapes=[pltpu.VMEM(*x) if isinstance(x, tuple) else x for x in scratch],
        compiler_params=pltpu.CompilerParams(vmem_limit_bytes=limit * 1024 * 1024),
        **more,
    )


def f32(*shape):
    return jax.ShapeDtypeStruct(shape, F32)


def bf16(*shape):
    return jax.ShapeDtypeStruct(shape, BF16)


EDGE_OUTS = (f32(2 * PAIRS, 256),) * 3 + (f32(ACQ, 256),) * 3
OWN_OUTS = EDGE_OUTS + (bf16(PAIRS, K), bf16(PAIRS, 3 * K), f32(PAIRS, 128))
OWN_SCRATCH = (
    ((3 * K, HALF * 256 + 128), BF16),
    ((2 * PAIRS, HALF * 256 + 128), F32),
    ((2 * PAIRS, 256), BF16),
    ((2 * PAIRS, 128), F32),
)
EDGE_SCRATCH = (
    ((3 * K, 512), BF16),
    ((2 * PAIRS, 512), F32),
    ((4 * PAIRS, 256), BF16),
    ((4 * PAIRS, 128), F32),
)
CHIP_SCRATCH = EDGE_SCRATCH + (((PAIRS, 3 * 128), BF16),)


def per_device(slc_re, slc_im, pairs):
    send = call(
        pack_kernel,
        f32(DEVS * CHUNK, 128),
        [HBM] * 3,
        (
            ((ROWS, ACQ_DEV, RG), F32),
            ((ROWS, ACQ_DEV, RG), F32),
            ((2, PAIR_DEV), jnp.int32),
            ((2 * HALF, ACQ_DEV, RG), F32),
            pltpu.SemaphoreType.DMA((3,)),
        ),
        limit=40,
        out_spec=VMEM,
    )(*[pltpu.with_memory_space_constraint(x, pltpu.HBM) for x in (jnp.transpose(slc_re, (1, 0, 2)), jnp.transpose(slc_im, (1, 0, 2)), pairs.T)])
    send = send.reshape(DEVS, CHUNK // 4, 4, 128)
    recv = lax.all_to_all(send, "acq", split_axis=0, concat_axis=0, tiled=True)
    recv = recv.reshape(DEVS * CHUNK, 128)
    chip, core = call(edges_kernel, (f32(2 * ACQ + 8, 128), f32(2 * ACQ, 128)), [VMEM])(recv)
    count = lax.axis_size("az")
    across = [(i, i + 1) for i in range(1, count - 1, 2)]
    inside = [(i, i + 1) for i in range(0, count, 2)]
    chip = lax.ppermute(chip, "az", across + [(j, i) for i, j in across])
    core = lax.ppermute(core, "az", inside + [(j, i) for i, j in inside])
    cost = [pl.CostEstimate(flops=n, bytes_accessed=n, transcendentals=0) for n in (10**3, 10**3)]
    own = call(own_kernel, OWN_OUTS, [VMEM], OWN_SCRATCH, cost_estimate=cost[0])(recv)
    up, down, turn, up_power, down_power, turn_power, pick_a, pick_b, value = own
    value = call(core_kernel, f32(PAIRS, 128), [VMEM] * 8, EDGE_SCRATCH, cost_estimate=cost[1])(
        core, down, turn, down_power, turn_power, pick_a, pick_b, value
    )
    result = call(chip_kernel, f32(2 * DEVS, 128), [VMEM] * 8, CHIP_SCRATCH)(
        chip, up, turn, up_power, turn_power, pick_a, pick_b, value
    )
    got = lax.all_to_all(result.reshape(DEVS, 2, 128), "acq", split_axis=0, concat_axis=0, tiled=True)
    outs = call(finish_kernel, (f32(32, 64),) * 3, [VMEM])(got.reshape(2 * DEVS, 128))
    return tuple(x.reshape(PAIR_DEV, 2, 64) for x in outs)


def solution(mesh):
    in_specs = (P("acq", "az", None), P("acq", "az", None), P("acq", None))
    out_specs = (P("acq", "az", None), P("acq", "az", None), P("acq", "az", None))
    return jax.shard_map(per_device, mesh=mesh, in_specs=in_specs, out_specs=out_specs, check_vma=False)
```

```python
import jax
import jax.numpy as jnp
from jax import lax
from jax.experimental import pallas as pl
from jax.experimental.pallas import tpu as pltpu
from jax.sharding import PartitionSpec as P

DEVS = 32
ACQ_DEV = 6
ACQ = DEVS * ACQ_DEV
PAIR_DEV = 16
PAIRS = DEVS * PAIR_DEV
ROWS = 10
HALF = 5
RG = 1280
STEP = 40
WIDE = STEP + 19
CHUNK = 60
K = 256
F32 = jnp.float32
BF16 = jnp.bfloat16
VMEM = pl.BlockSpec(memory_space=pltpu.VMEM)
HBM = pl.BlockSpec(memory_space=pltpu.HBM)
BIG = 3.38e38
PART = 8 * ACQ_DEV


def lanes_of(shape):
    return lax.broadcasted_iota(jnp.int32, shape, len(shape) - 1)


def odd_row():
    return lax.axis_index("az") & 1


def pack_kernel(re_hbm, im_hbm, pairs_hbm, chunks, re_ref, im_ref, pairs_ref, later, sems):
    odd = odd_row()
    copies = [
        pltpu.make_async_copy(source, target, sems.at[n])
        for n, (source, target) in enumerate(((pairs_hbm, pairs_ref), (re_hbm, re_ref), (im_hbm, im_ref)))
    ]
    for copy in copies:
        copy.start()
    lane = lanes_of((ACQ_DEV, 128))
    wide = lanes_of((3 * ACQ_DEV, 128))
    copies[0].wait()
    acq = pairs_ref[...]
    group = (acq * 171) >> 10
    local = (acq - ACQ_DEV * group) * 8 + (group & 7)
    order = lax.broadcasted_iota(jnp.int32, (2, PAIR_DEV), 0)
    index = (local + jnp.where(order == 0, 0, (group >> 3) * PART)).astype(F32)
    square = (PAIR_DEV, PAIR_DEV)
    diagonal = lax.broadcasted_iota(jnp.int32, square, 0) == lax.broadcasted_iota(jnp.int32, square, 1)
    columns = [
        jnp.sum(jnp.where(diagonal, jnp.broadcast_to(index[w : w + 1, :], square), 0.0), axis=1, keepdims=True)
        for w in range(2)
    ]
    none = jnp.zeros((3 * ACQ_DEV - PAIR_DEV, 128), F32)
    first, second = [jnp.concatenate([jnp.broadcast_to(x, (PAIR_DEV, 128)), none], axis=0) for x in columns]
    marks = jnp.where(wide == 60, first, jnp.where(wide == 61, second, 0.0))
    marks = [marks[n * ACQ_DEV : (n + 1) * ACQ_DEV] for n in range(3)]
    tiles = RG // 128
    for part, ref in enumerate((re_ref, im_ref)):
        copies[1 + part].wait()
        for r in range(HALF):
            row = r + HALF + odd * (9 - 2 * (r + HALF))
            for t in range(tiles):
                x = ref[row, :, t * 128 : (t + 1) * 128]
                later[part * HALF + r, :, t * 128 : (t + 1) * 128] = pltpu.roll(x, 64, 1)
    for d in range(DEVS):
        start = STEP * d - 10
        k = start // 128
        off = start - 128 * k
        spans = []
        for t, low, high in ((k, off, min(128, off + WIDE)), (k + 1, 0, off + WIDE - 128)):
            if low < high and 0 <= t < tiles:
                spans.append((t, False, low, high))
                shifted = [(low + 64, min(high + 64, 128)), (max(low + 64, 128) - 128, high + 64 - 128)]
                spans += [(t, True, x, y) for x, y in shifted if x < y]
        masks = [(lane >= low) & (lane < high) for _, _, low, high in spans]
        for part, ref in enumerate((re_ref, im_ref)):
            for r in range(HALF):
                row = r + odd * (9 - 2 * r)
                mixed = jnp.zeros((ACQ_DEV, 128), F32)
                for (t, shifted, _, _), mask in zip(spans, masks):
                    at = slice(t * 128, (t + 1) * 128)
                    mixed = jnp.where(mask, later[part * HALF + r, :, at] if shifted else ref[row, :, at], mixed)
                top = d * CHUNK + (part * HALF + r) * ACQ_DEV
                mixed = pltpu.roll(mixed, 128 - off, 1) if off else mixed
                if part == 0 and r < 3:
                    mixed = mixed + marks[r]
                chunks[top : top + ACQ_DEV, :] = mixed


def acq_rows(recv_ref, part, r):
    base = (part * HALF + r) * ACQ_DEV
    return jnp.concatenate(
        [recv_ref[pl.ds(base + a + 8 * g * CHUNK, 8, stride=CHUNK), :] for g in range(4) for a in range(ACQ_DEV)],
        axis=0,
    )


def chip_edge_kernel(recv_ref, out_ref):
    lane = lanes_of((ACQ, 128))
    for part in range(2):
        v0, v1 = [acq_rows(recv_ref, part, r) for r in (0, 1)]
        out_ref[part * ACQ : (part + 1) * ACQ, :] = jnp.where(lane < 64, v0, pltpu.roll(v1, 64, 1))
    out_ref[2 * ACQ :, :] = jnp.zeros((8, 128), F32)


def core_edge_kernel(recv_ref, out_ref):
    lane = lanes_of((ACQ, 128))
    for part in range(2):
        v3, v4 = [acq_rows(recv_ref, part, r) for r in (3, 4)]
        out_ref[part * ACQ : (part + 1) * ACQ, :] = jnp.where(lane < 64, pltpu.roll(v3, 64, 1), v4)


def pieces_of(x, count):
    out = []
    for n in range(count):
        piece = x.astype(BF16)
        out.append(piece)
        if n + 1 < count:
            x = x - piece.astype(F32)
    return out


def clamp(x):
    return jnp.minimum(jnp.maximum(x, -BIG), BIG)


def dot(x, y):
    return jnp.dot(x, y, preferred_element_type=F32)


def fill(table):
    for p in range(3):
        table[p * K + ACQ : (p + 1) * K, :] = jnp.zeros((K - ACQ, table.shape[1]), BF16)


def enter(table, x, at):
    for p, piece in enumerate(pieces_of(clamp(x), 3)):
        table[p * K : p * K + ACQ, at : at + x.shape[1]] = piece


def along_range():
    shape = (128, 128)
    k = lax.broadcasted_iota(jnp.int32, shape, 0)
    n = lax.broadcasted_iota(jnp.int32, shape, 1)
    c = n & 63
    first = jnp.where(c < STEP, c, jnp.where(c < STEP + 4, 10 + 20 * (c & 1), -1000))
    sample = k & 63
    inside = ((k >> 6) == (n >> 6)) & (sample >= first) & (sample <= first + 19)
    box = jnp.where(inside, 1.0, 0.0).astype(BF16)
    return jnp.concatenate([box, box], axis=0)


def choose(pick_a, pick_b, table, picked, at, width, parts):
    columns = slice(at, at + width)
    picked[PAIRS:, columns] = dot(pick_b[:, : parts * K], table[: parts * K, columns])
    for g in range(4):
        few = jnp.concatenate([table[p * K + g * PART : p * K + (g + 1) * PART, columns] for p in range(3)], axis=0)
        picked[128 * g : 128 * (g + 1), columns] = dot(pick_a[128 * g : 128 * (g + 1), : 3 * PART], few)


def cross(picked, top, count):
    fields = [[], []]
    for t in range(count):
        ra = picked[pl.ds(top, 16), t * 256 : t * 256 + 128]
        ia = picked[pl.ds(top, 16), t * 256 + 128 : t * 256 + 256]
        rb = picked[pl.ds(top + PAIRS, 16), t * 256 : t * 256 + 128]
        ib = picked[pl.ds(top + PAIRS, 16), t * 256 + 128 : t * 256 + 256]
        fields[0].append(ra * rb + ia * ib)
        fields[1].append(ia * rb - ra * ib)
    return fields


def own_rows(v):
    v0, v1, v2, v3, v4 = v
    low = lanes_of(v0.shape) < 64
    next_one = pltpu.roll(jnp.where(low, v4, v0), 64, 1)
    next_two = next_one + pltpu.roll(jnp.where(low, v3, v1), 64, 1)
    v12, v34 = v1 + v2, v3 + v4
    v012, v234 = v0 + v12, v2 + v34
    return v012, v012 + v3, v012 + v34, v1 + v234, v234, next_two, next_one


def edge_rows(sums, turned, here, edge, low):
    inside = (lanes_of(edge.shape) < 64) == low
    two = edge + pltpu.roll(edge, 64, 1)
    near = sums[here, 0:128] + jnp.where(inside, two, turned[here, 0:128])
    return near, sums[here, 128:256] + jnp.where(inside, edge, turned[here, 128:256])


def store_terms(terms, top, x):
    for n, piece in enumerate(pieces_of(x, 2)):
        terms[pl.ds(top, 16), n * 128 : (n + 1) * 128] = piece


def enter_power(table, x, box, at):
    high, mid, low = pieces_of(x, 3)
    enter(table, dot(jnp.concatenate([high, mid], axis=1), box) + dot(low, box[:128]), at)


def coherence_of(total, picked, top, row, at):
    x0 = total[pl.ds(top + 2 * row * PAIRS, 16), :]
    x1 = total[pl.ds(top + (2 * row + 1) * PAIRS, 16), :]
    wa = picked[pl.ds(top, 16), at : at + 128]
    wb = picked[pl.ds(top + PAIRS, 16), at : at + 128]
    inverse = lax.rsqrt(wa * wb + 1e-06)
    num = x0 * x0 + x1 * x1
    return num * lax.rsqrt(jnp.maximum(num, 1e-37)) * inverse, x0, x1, inverse


def for_pairs(body):
    def step(g, carry):
        body(pl.multiple_of(16 * g, 16))
        return carry

    lax.fori_loop(0, PAIRS // 16, step, 0, unroll=True)


def own_kernel(
    recv_ref, up_ref, down_ref, turn_ref, up_power, down_power, turn_power, pick_a, pick_b, value_ref, table, picked, terms, total
):
    lane = lanes_of((128, K))
    few = lane - PART * ((lane * 342) >> 14)
    for g in range(4):
        head = jnp.concatenate([recv_ref[pl.ds(8 * g * CHUNK + p, 8, stride=CHUNK), :] for p in range(PAIR_DEV)], axis=0)
        rows = slice(128 * g, 128 * (g + 1))
        index = jnp.broadcast_to(head[:, 60:61], (128, K))
        pick_a[rows, :] = jnp.where(index == few.astype(F32), 1.0, 0.0).astype(BF16)
        index = jnp.broadcast_to(head[:, 61:62], (128, K))
        hot = jnp.where(index == lane.astype(F32), 1.0, 0.0).astype(BF16)
        for p in range(3):
            pick_b[rows, p * K : (p + 1) * K] = hot
    fill(table)
    box = along_range()
    squares = []
    for t in range(HALF):
        parts = [acq_rows(recv_ref, part, t) for part in range(2)]
        for part, x in enumerate(parts):
            enter(table, x, t * 256 + part * 128)
        squares.append(parts[0] * parts[0] + parts[1] * parts[1])
        choose(pick_a, pick_b, table, picked, t * 256, 256, 2)
    sums = own_rows(squares)
    up_power[:, 0:128], up_power[:, 128:256] = sums[0], sums[1]
    down_power[:, 0:128], down_power[:, 128:256] = sums[4], sums[3]
    turn_power[:, 0:128], turn_power[:, 128:256] = sums[5], sums[6]
    enter_power(table, sums[2], box, HALF * 256)
    choose(pick_a, pick_b, table, picked, HALF * 256, 128, 3)

    def rows(top):
        for f, field in enumerate(cross(picked, top, HALF)):
            x = own_rows(field)
            here = pl.ds(top + f * PAIRS, 16)
            up_ref[here, 0:128], up_ref[here, 128:256] = x[0], x[1]
            down_ref[here, 0:128], down_ref[here, 128:256] = x[4], x[3]
            turn_ref[here, 0:128], turn_ref[here, 128:256] = x[5], x[6]
            store_terms(terms, top + f * PAIRS, x[2])

    for_pairs(rows)
    total[...] = dot(terms[...], box)
    lane16 = lanes_of((16, 128)) & 63

    def some(top):
        size, x0, x1, inverse = coherence_of(total, picked, top, 0, HALF * 256)
        value_ref[pl.ds(top, 16), :] = jnp.where(lane16 < STEP, size, jnp.where(lane16 < STEP + 2, x0, x1) * inverse)

    for_pairs(some)


def edge_coherence(edge_ref, sums, powers, pick_a, pick_b, table, picked, terms, total, low):
    fill(table)
    box = along_range()
    parts = [edge_ref[part * ACQ : (part + 1) * ACQ, :] for part in range(2)]
    for part, x in enumerate(parts):
        enter(table, x, part * 128)
    square = parts[0] * parts[0] + parts[1] * parts[1]
    for n, x in enumerate(edge_rows(*powers, slice(0, ACQ), square, low)):
        enter_power(table, x, box, 256 + n * 128)
    choose(pick_a, pick_b, table, picked, 0, 256, 2)
    choose(pick_a, pick_b, table, picked, 256, 256, 3)

    def rows(top):
        for f, field in enumerate(cross(picked, top, 1)):
            here = pl.ds(top + f * PAIRS, 16)
            for n, x in enumerate(edge_rows(*sums, here, field[0], low)):
                store_terms(terms, top + (2 * n + f) * PAIRS, x)

    for_pairs(rows)
    total[...] = dot(terms[...], box)


def edge_value(value_ref, total, picked, top):
    size = coherence_of(total, picked, top, 0, 256)[0] + coherence_of(total, picked, top, 1, 384)[0]
    return value_ref[pl.ds(top, 16), :] + jnp.where((lanes_of(size.shape) & 63) < STEP, size, 0.0)


def core_kernel(core_ref, sums_ref, turn_ref, power_ref, turn_power, pick_a, pick_b, value_ref, out_ref, table, picked, terms, total):
    sums, powers = (sums_ref, turn_ref), (power_ref, turn_power)
    edge_coherence(core_ref, sums, powers, pick_a, pick_b, table, picked, terms, total, False)

    def some(top):
        out_ref[pl.ds(top, 16), :] = edge_value(value_ref, total, picked, top)

    for_pairs(some)


def chip_kernel(chip_ref, sums_ref, turn_ref, power_ref, turn_power, pick_a, pick_b, value_ref, out_ref, table, picked, terms, total, ends):
    sums, powers = (sums_ref, turn_ref), (power_ref, turn_power)
    edge_coherence(chip_ref, sums, powers, pick_a, pick_b, table, picked, terms, total, True)

    def some(top):
        for p, piece in enumerate(pieces_of(edge_value(value_ref, total, picked, top), 3)):
            ends[pl.ds(top, 16), p * 128 : (p + 1) * 128] = piece

    for_pairs(some)

    n = lax.broadcasted_iota(jnp.int32, (128, 256), 0)
    m = lax.broadcasted_iota(jnp.int32, (128, 256), 1)
    c, j, o = n & 63, m >> 7, (m >> 5) & 3
    first = jnp.where(o == 0, 20 * j, jnp.where(o == 3, 1000, STEP - 2 + 2 * o + j))
    last = first + jnp.where(o == 0, 19, 0)
    same = ((n >> 6) == ((m & 1) ^ odd_row())) & (c >= first) & (c <= last)
    spread = jnp.where(same, 1.0, 0.0).astype(BF16)
    result = dot(ends[...], jnp.concatenate([spread] * 3, axis=0))
    owner = (lanes_of((8, 128)) >> 1) & 15
    for j in range(2):
        for g in range(4):
            out = None
            for p in range(PAIR_DEV):
                top = 128 * g + 8 * p
                rows_p = result[top : top + 8, j * 128 : (j + 1) * 128]
                out = rows_p if out is None else jnp.where(owner == p, rows_p, out)
            out_ref[pl.ds(16 * g + j, 8, stride=2), :] = out


def finish_kernel(got_ref, coh_ref, re_ref, im_ref):
    turned = jnp.transpose(got_ref[...])
    coh_ref[...] = turned[0:32] * 0.01
    re_ref[...] = turned[32:64]
    im_ref[...] = turned[64:96]


def call(kernel, outs, specs, scratch=(), limit=40, out_spec=VMEM, **more):
    return pl.pallas_call(
        kernel,
        out_shape=outs,
        in_specs=specs,
        out_specs=jax.tree.map(lambda _: out_spec, outs),
        scratch_shapes=[pltpu.VMEM(*x) if isinstance(x, tuple) else x for x in scratch],
        compiler_params=pltpu.CompilerParams(vmem_limit_bytes=limit * 1024 * 1024),
        **more,
    )


def f32(*shape):
    return jax.ShapeDtypeStruct(shape, F32)


def bf16(*shape):
    return jax.ShapeDtypeStruct(shape, BF16)


EDGE_OUTS = (f32(2 * PAIRS, 256),) * 3 + (f32(ACQ, 256),) * 3
OWN_OUTS = EDGE_OUTS + (bf16(PAIRS, K), bf16(PAIRS, 3 * K), f32(PAIRS, 128))
OWN_SCRATCH = (
    ((3 * K, HALF * 256 + 128), BF16),
    ((2 * PAIRS, HALF * 256 + 128), F32),
    ((2 * PAIRS, 256), BF16),
    ((2 * PAIRS, 128), F32),
)
EDGE_SCRATCH = (
    ((3 * K, 512), BF16),
    ((2 * PAIRS, 512), F32),
    ((4 * PAIRS, 256), BF16),
    ((4 * PAIRS, 128), F32),
)
CHIP_SCRATCH = EDGE_SCRATCH + (((PAIRS, 3 * 128), BF16),)


def per_device(slc_re, slc_im, pairs):
    send = call(
        pack_kernel,
        f32(DEVS * CHUNK, 128),
        [HBM] * 3,
        (
            ((ROWS, ACQ_DEV, RG), F32),
            ((ROWS, ACQ_DEV, RG), F32),
            ((2, PAIR_DEV), jnp.int32),
            ((2 * HALF, ACQ_DEV, RG), F32),
            pltpu.SemaphoreType.DMA((3,)),
        ),
        limit=40,
        out_spec=VMEM,
    )(*[pltpu.with_memory_space_constraint(x, pltpu.HBM) for x in (jnp.transpose(slc_re, (1, 0, 2)), jnp.transpose(slc_im, (1, 0, 2)), pairs.T)])
    send = send.reshape(DEVS, CHUNK // 4, 4, 128)
    recv = lax.all_to_all(send, "acq", split_axis=0, concat_axis=0, tiled=True)
    recv = recv.reshape(DEVS * CHUNK, 128)
    chip = call(chip_edge_kernel, f32(2 * ACQ + 8, 128), [VMEM])(recv)
    core = call(core_edge_kernel, f32(2 * ACQ, 128), [VMEM])(recv)
    count = lax.axis_size("az")
    across = [(i, i + 1) for i in range(1, count - 1, 2)]
    inside = [(i, i + 1) for i in range(0, count, 2)]
    chip = lax.ppermute(chip, "az", across + [(j, i) for i, j in across])
    core = lax.ppermute(core, "az", inside + [(j, i) for i, j in inside])
    cost = [pl.CostEstimate(flops=n, bytes_accessed=n, transcendentals=0) for n in (10**3, 10**3)]
    own = call(own_kernel, OWN_OUTS, [VMEM], OWN_SCRATCH, cost_estimate=cost[0])(recv)
    up, down, turn, up_power, down_power, turn_power, pick_a, pick_b, value = own
    value = call(core_kernel, f32(PAIRS, 128), [VMEM] * 8, EDGE_SCRATCH, cost_estimate=cost[1])(
        core, down, turn, down_power, turn_power, pick_a, pick_b, value
    )
    result = call(chip_kernel, f32(2 * DEVS, 128), [VMEM] * 8, CHIP_SCRATCH)(
        chip, up, turn, up_power, turn_power, pick_a, pick_b, value
    )
    got = lax.all_to_all(result.reshape(DEVS, 2, 128), "acq", split_axis=0, concat_axis=0, tiled=True)
    outs = call(finish_kernel, (f32(32, 64),) * 3, [VMEM])(got.reshape(2 * DEVS, 128))
    return tuple(x.reshape(PAIR_DEV, 2, 64) for x in outs)


def solution(mesh):
    in_specs = (P("acq", "az", None), P("acq", "az", None), P("acq", None))
    out_specs = (P("acq", "az", None), P("acq", "az", None), P("acq", "az", None))
    return jax.shard_map(per_device, mesh=mesh, in_specs=in_specs, out_specs=out_specs, check_vma=False)
```

```python
import jax
import jax.numpy as jnp
from jax import lax
from jax.experimental import pallas as pl
from jax.experimental.pallas import tpu as pltpu
from jax.sharding import PartitionSpec as P

DEVS = 32
ACQ_DEV = 6
ACQ = DEVS * ACQ_DEV
PAIR_DEV = 16
PAIRS = DEVS * PAIR_DEV
ROWS = 10
HALF = 5
RG = 1280
STEP = 40
WIDE = STEP + 19
CHUNK = 60
K = 256
F32 = jnp.float32
BF16 = jnp.bfloat16
VMEM = pl.BlockSpec(memory_space=pltpu.VMEM)
HBM = pl.BlockSpec(memory_space=pltpu.HBM)
BIG = 3.38e38
PART = 8 * ACQ_DEV


def lanes_of(shape):
    return lax.broadcasted_iota(jnp.int32, shape, len(shape) - 1)


def odd_row():
    return lax.axis_index("az") & 1


def pack_kernel(re_hbm, im_hbm, pairs_hbm, chunks, re_ref, im_ref, pairs_ref, later, sems):
    odd = odd_row()
    copies = [
        pltpu.make_async_copy(source, target, sems.at[n])
        for n, (source, target) in enumerate(((pairs_hbm, pairs_ref), (re_hbm, re_ref), (im_hbm, im_ref)))
    ]
    for copy in copies:
        copy.start()
    lane = lanes_of((ACQ_DEV, 128))
    wide = lanes_of((3 * ACQ_DEV, 128))
    copies[0].wait()
    acq = pairs_ref[...]
    group = (acq * 171) >> 10
    local = (acq - ACQ_DEV * group) * 8 + (group & 7)
    order = lax.broadcasted_iota(jnp.int32, (2, PAIR_DEV), 0)
    index = (local + jnp.where(order == 0, 0, (group >> 3) * PART)).astype(F32)
    square = (PAIR_DEV, PAIR_DEV)
    diagonal = lax.broadcasted_iota(jnp.int32, square, 0) == lax.broadcasted_iota(jnp.int32, square, 1)
    columns = [
        jnp.sum(jnp.where(diagonal, jnp.broadcast_to(index[w : w + 1, :], square), 0.0), axis=1, keepdims=True)
        for w in range(2)
    ]
    none = jnp.zeros((3 * ACQ_DEV - PAIR_DEV, 128), F32)
    first, second = [jnp.concatenate([jnp.broadcast_to(x, (PAIR_DEV, 128)), none], axis=0) for x in columns]
    marks = jnp.where(wide == 60, first, jnp.where(wide == 61, second, 0.0))
    marks = [marks[n * ACQ_DEV : (n + 1) * ACQ_DEV] for n in range(3)]
    tiles = RG // 128
    for part, ref in enumerate((re_ref, im_ref)):
        copies[1 + part].wait()
        for r in range(HALF):
            row = r + HALF + odd * (9 - 2 * (r + HALF))
            for t in range(tiles):
                x = ref[row, :, t * 128 : (t + 1) * 128]
                later[part * HALF + r, :, t * 128 : (t + 1) * 128] = pltpu.roll(x, 64, 1)
    for d in range(DEVS):
        start = STEP * d - 10
        k = start // 128
        off = start - 128 * k
        spans = []
        for t, low, high in ((k, off, min(128, off + WIDE)), (k + 1, 0, off + WIDE - 128)):
            if low < high and 0 <= t < tiles:
                spans.append((t, False, low, high))
                shifted = [(low + 64, min(high + 64, 128)), (max(low + 64, 128) - 128, high + 64 - 128)]
                spans += [(t, True, x, y) for x, y in shifted if x < y]
        masks = [(lane >= low) & (lane < high) for _, _, low, high in spans]
        for part, ref in enumerate((re_ref, im_ref)):
            for r in range(HALF):
                row = r + odd * (9 - 2 * r)
                mixed = jnp.zeros((ACQ_DEV, 128), F32)
                for (t, shifted, _, _), mask in zip(spans, masks):
                    at = slice(t * 128, (t + 1) * 128)
                    mixed = jnp.where(mask, later[part * HALF + r, :, at] if shifted else ref[row, :, at], mixed)
                top = d * CHUNK + (part * HALF + r) * ACQ_DEV
                mixed = pltpu.roll(mixed, 128 - off, 1) if off else mixed
                if part == 0 and r < 3:
                    mixed = mixed + marks[r]
                chunks[top : top + ACQ_DEV, :] = mixed


def acq_rows(recv_ref, part, r):
    base = (part * HALF + r) * ACQ_DEV
    return jnp.concatenate(
        [recv_ref[pl.ds(base + a + 8 * g * CHUNK, 8, stride=CHUNK), :] for g in range(4) for a in range(ACQ_DEV)],
        axis=0,
    )


def edges_kernel(recv_ref, chip_ref, core_ref):
    lane = lanes_of((ACQ, 128))
    for part in range(2):
        v0, v1, v3, v4 = [acq_rows(recv_ref, part, r) for r in (0, 1, 3, 4)]
        rows = slice(part * ACQ, (part + 1) * ACQ)
        chip_ref[rows, :] = jnp.where(lane < 64, v0, pltpu.roll(v1, 64, 1))
        core_ref[rows, :] = jnp.where(lane < 64, pltpu.roll(v3, 64, 1), v4)
    chip_ref[2 * ACQ :, :] = jnp.zeros((8, 128), F32)


def pieces_of(x, count):
    out = []
    for n in range(count):
        piece = x.astype(BF16)
        out.append(piece)
        if n + 1 < count:
            x = x - piece.astype(F32)
    return out


def clamp(x):
    return jnp.minimum(jnp.maximum(x, -BIG), BIG)


def dot(x, y):
    return jnp.dot(x, y, preferred_element_type=F32)


def fill(table):
    for p in range(3):
        table[p * K + ACQ : (p + 1) * K, :] = jnp.zeros((K - ACQ, table.shape[1]), BF16)


def enter(table, x, at):
    for p, piece in enumerate(pieces_of(clamp(x), 3)):
        table[p * K : p * K + ACQ, at : at + x.shape[1]] = piece


def along_range():
    shape = (128, 128)
    k = lax.broadcasted_iota(jnp.int32, shape, 0)
    n = lax.broadcasted_iota(jnp.int32, shape, 1)
    c = n & 63
    first = jnp.where(c < STEP, c, jnp.where(c < STEP + 4, 10 + 20 * (c & 1), -1000))
    sample = k & 63
    inside = ((k >> 6) == (n >> 6)) & (sample >= first) & (sample <= first + 19)
    box = jnp.where(inside, 1.0, 0.0).astype(BF16)
    return jnp.concatenate([box, box], axis=0)


def choose(pick_a, pick_b, table, picked, at, width, parts):
    columns = slice(at, at + width)
    picked[PAIRS:, columns] = dot(pick_b[:, : parts * K], table[: parts * K, columns])
    for g in range(4):
        few = jnp.concatenate([table[p * K + g * PART : p * K + (g + 1) * PART, columns] for p in range(3)], axis=0)
        picked[128 * g : 128 * (g + 1), columns] = dot(pick_a[128 * g : 128 * (g + 1), : 3 * PART], few)


def cross(picked, top, count):
    fields = [[], []]
    for t in range(count):
        ra = picked[pl.ds(top, 16), t * 256 : t * 256 + 128]
        ia = picked[pl.ds(top, 16), t * 256 + 128 : t * 256 + 256]
        rb = picked[pl.ds(top + PAIRS, 16), t * 256 : t * 256 + 128]
        ib = picked[pl.ds(top + PAIRS, 16), t * 256 + 128 : t * 256 + 256]
        fields[0].append(ra * rb + ia * ib)
        fields[1].append(ia * rb - ra * ib)
    return fields


def own_rows(v):
    v0, v1, v2, v3, v4 = v
    low = lanes_of(v0.shape) < 64
    next_one = pltpu.roll(jnp.where(low, v4, v0), 64, 1)
    next_two = next_one + pltpu.roll(jnp.where(low, v3, v1), 64, 1)
    v12, v34 = v1 + v2, v3 + v4
    v012, v234 = v0 + v12, v2 + v34
    return [
        v012 + jnp.where(low, 0.0, next_two),
        (v012 + v3) + jnp.where(low, 0.0, next_one),
        v012 + v34,
        (v1 + v234) + jnp.where(low, next_one, 0.0),
        v234 + jnp.where(low, next_two, 0.0),
    ]


def edge_rows(near, far, edge, low):
    inside = (lanes_of(edge.shape) < 64) == low
    return near + jnp.where(inside, edge + pltpu.roll(edge, 64, 1), 0.0), far + jnp.where(inside, edge, 0.0)


def store_terms(terms, top, x):
    for n, piece in enumerate(pieces_of(x, 2)):
        terms[pl.ds(top, 16), n * 128 : (n + 1) * 128] = piece


def enter_power(table, x, box, at):
    high, mid, low = pieces_of(x, 3)
    enter(table, dot(jnp.concatenate([high, mid], axis=1), box) + dot(low, box[:128]), at)


def coherence_of(total, picked, top, row, at):
    x0 = total[pl.ds(top + 2 * row * PAIRS, 16), :]
    x1 = total[pl.ds(top + (2 * row + 1) * PAIRS, 16), :]
    wa = picked[pl.ds(top, 16), at : at + 128]
    wb = picked[pl.ds(top + PAIRS, 16), at : at + 128]
    inverse = lax.rsqrt(wa * wb + 1e-06)
    num = x0 * x0 + x1 * x1
    return num * lax.rsqrt(jnp.maximum(num, 1e-37)) * inverse, x0, x1, inverse


def for_pairs(body):
    def step(g, carry):
        body(pl.multiple_of(16 * g, 16))
        return carry

    lax.fori_loop(0, PAIRS // 16, step, 0, unroll=True)


def own_kernel(
    recv_ref, up_ref, down_ref, up_power, down_power, pick_a, pick_b, value_ref, table, picked, terms, total
):
    lane = lanes_of((128, K))
    few = lane - PART * ((lane * 342) >> 14)
    for g in range(4):
        head = jnp.concatenate([recv_ref[pl.ds(8 * g * CHUNK + p, 8, stride=CHUNK), :] for p in range(PAIR_DEV)], axis=0)
        rows = slice(128 * g, 128 * (g + 1))
        index = jnp.broadcast_to(head[:, 60:61], (128, K))
        pick_a[rows, :] = jnp.where(index == few.astype(F32), 1.0, 0.0).astype(BF16)
        index = jnp.broadcast_to(head[:, 61:62], (128, K))
        hot = jnp.where(index == lane.astype(F32), 1.0, 0.0).astype(BF16)
        for p in range(3):
            pick_b[rows, p * K : (p + 1) * K] = hot
    fill(table)
    box = along_range()
    squares = []
    for t in range(HALF):
        parts = [acq_rows(recv_ref, part, t) for part in range(2)]
        for part, x in enumerate(parts):
            enter(table, x, t * 256 + part * 128)
        squares.append(parts[0] * parts[0] + parts[1] * parts[1])
        choose(pick_a, pick_b, table, picked, t * 256, 256, 2)
    sums = own_rows(squares)
    up_power[:, 0:128], up_power[:, 128:256] = sums[0], sums[1]
    down_power[:, 0:128], down_power[:, 128:256] = sums[4], sums[3]
    enter_power(table, sums[2], box, HALF * 256)
    choose(pick_a, pick_b, table, picked, HALF * 256, 128, 3)

    def rows(top):
        for f, field in enumerate(cross(picked, top, HALF)):
            x = own_rows(field)
            here = pl.ds(top + f * PAIRS, 16)
            up_ref[here, 0:128], up_ref[here, 128:256] = x[0], x[1]
            down_ref[here, 0:128], down_ref[here, 128:256] = x[4], x[3]
            store_terms(terms, top + f * PAIRS, x[2])

    for_pairs(rows)
    total[...] = dot(terms[...], box)
    lane16 = lanes_of((16, 128)) & 63

    def some(top):
        size, x0, x1, inverse = coherence_of(total, picked, top, 0, HALF * 256)
        value_ref[pl.ds(top, 16), :] = jnp.where(lane16 < STEP, size, jnp.where(lane16 < STEP + 2, x0, x1) * inverse)

    for_pairs(some)


def edge_coherence(edge_ref, sums_ref, power_ref, pick_a, pick_b, table, picked, terms, total, low):
    fill(table)
    box = along_range()
    parts = [edge_ref[part * ACQ : (part + 1) * ACQ, :] for part in range(2)]
    for part, x in enumerate(parts):
        enter(table, x, part * 128)
    square = parts[0] * parts[0] + parts[1] * parts[1]
    for n, x in enumerate(edge_rows(power_ref[:, 0:128], power_ref[:, 128:256], square, low)):
        enter_power(table, x, box, 256 + n * 128)
    choose(pick_a, pick_b, table, picked, 0, 256, 2)
    choose(pick_a, pick_b, table, picked, 256, 256, 3)

    def rows(top):
        for f, field in enumerate(cross(picked, top, 1)):
            here = pl.ds(top + f * PAIRS, 16)
            for n, x in enumerate(edge_rows(sums_ref[here, 0:128], sums_ref[here, 128:256], field[0], low)):
                store_terms(terms, top + (2 * n + f) * PAIRS, x)

    for_pairs(rows)
    total[...] = dot(terms[...], box)


def edge_value(value_ref, total, picked, top):
    size = coherence_of(total, picked, top, 0, 256)[0] + coherence_of(total, picked, top, 1, 384)[0]
    return value_ref[pl.ds(top, 16), :] + jnp.where((lanes_of(size.shape) & 63) < STEP, size, 0.0)


def core_kernel(core_ref, sums_ref, power_ref, pick_a, pick_b, value_ref, out_ref, table, picked, terms, total):
    edge_coherence(core_ref, sums_ref, power_ref, pick_a, pick_b, table, picked, terms, total, False)

    def some(top):
        out_ref[pl.ds(top, 16), :] = edge_value(value_ref, total, picked, top)

    for_pairs(some)


def chip_kernel(chip_ref, sums_ref, power_ref, pick_a, pick_b, value_ref, out_ref, table, picked, terms, total, ends):
    edge_coherence(chip_ref, sums_ref, power_ref, pick_a, pick_b, table, picked, terms, total, True)

    def some(top):
        for p, piece in enumerate(pieces_of(edge_value(value_ref, total, picked, top), 3)):
            ends[pl.ds(top, 16), p * 128 : (p + 1) * 128] = piece

    for_pairs(some)

    n = lax.broadcasted_iota(jnp.int32, (128, 256), 0)
    m = lax.broadcasted_iota(jnp.int32, (128, 256), 1)
    c, j, o = n & 63, m >> 7, (m >> 5) & 3
    first = jnp.where(o == 0, 20 * j, jnp.where(o == 3, 1000, STEP - 2 + 2 * o + j))
    last = first + jnp.where(o == 0, 19, 0)
    same = ((n >> 6) == ((m & 1) ^ odd_row())) & (c >= first) & (c <= last)
    spread = jnp.where(same, 1.0, 0.0).astype(BF16)
    result = dot(ends[...], jnp.concatenate([spread] * 3, axis=0))
    owner = (lanes_of((8, 128)) >> 1) & 15
    for j in range(2):
        for g in range(4):
            out = None
            for p in range(PAIR_DEV):
                top = 128 * g + 8 * p
                rows_p = result[top : top + 8, j * 128 : (j + 1) * 128]
                out = rows_p if out is None else jnp.where(owner == p, rows_p, out)
            out_ref[pl.ds(16 * g + j, 8, stride=2), :] = out


def finish_kernel(got_ref, coh_ref, re_ref, im_ref):
    turned = jnp.transpose(got_ref[...])
    coh_ref[...] = turned[0:32] * 0.01
    re_ref[...] = turned[32:64]
    im_ref[...] = turned[64:96]


def call(kernel, outs, specs, scratch=(), limit=40, out_spec=VMEM, **more):
    return pl.pallas_call(
        kernel,
        out_shape=outs,
        in_specs=specs,
        out_specs=jax.tree.map(lambda _: out_spec, outs),
        scratch_shapes=[pltpu.VMEM(*x) if isinstance(x, tuple) else x for x in scratch],
        compiler_params=pltpu.CompilerParams(vmem_limit_bytes=limit * 1024 * 1024),
        **more,
    )


def f32(*shape):
    return jax.ShapeDtypeStruct(shape, F32)


def bf16(*shape):
    return jax.ShapeDtypeStruct(shape, BF16)


EDGE_OUTS = (f32(2 * PAIRS, 256),) * 2 + (f32(ACQ, 256),) * 2
OWN_OUTS = EDGE_OUTS + (bf16(PAIRS, K), bf16(PAIRS, 3 * K), f32(PAIRS, 128))
OWN_SCRATCH = (
    ((3 * K, HALF * 256 + 128), BF16),
    ((2 * PAIRS, HALF * 256 + 128), F32),
    ((2 * PAIRS, 256), BF16),
    ((2 * PAIRS, 128), F32),
)
EDGE_SCRATCH = (
    ((3 * K, 512), BF16),
    ((2 * PAIRS, 512), F32),
    ((4 * PAIRS, 256), BF16),
    ((4 * PAIRS, 128), F32),
)
CHIP_SCRATCH = EDGE_SCRATCH + (((PAIRS, 3 * 128), BF16),)


def per_device(slc_re, slc_im, pairs):
    send = call(
        pack_kernel,
        f32(DEVS * CHUNK, 128),
        [HBM] * 3,
        (
            ((ROWS, ACQ_DEV, RG), F32),
            ((ROWS, ACQ_DEV, RG), F32),
            ((2, PAIR_DEV), jnp.int32),
            ((2 * HALF, ACQ_DEV, RG), F32),
            pltpu.SemaphoreType.DMA((3,)),
        ),
        limit=40,
        out_spec=VMEM,
    )(*[pltpu.with_memory_space_constraint(x, pltpu.HBM) for x in (jnp.transpose(slc_re, (1, 0, 2)), jnp.transpose(slc_im, (1, 0, 2)), pairs.T)])
    send = send.reshape(DEVS, CHUNK // 4, 4, 128)
    recv = lax.all_to_all(send, "acq", split_axis=0, concat_axis=0, tiled=True)
    recv = recv.reshape(DEVS * CHUNK, 128)
    chip, core = call(edges_kernel, (f32(2 * ACQ + 8, 128), f32(2 * ACQ, 128)), [VMEM])(recv)
    count = lax.axis_size("az")
    across = [(i, i + 1) for i in range(1, count - 1, 2)]
    inside = [(i, i + 1) for i in range(0, count, 2)]
    chip = lax.ppermute(chip, "az", across + [(j, i) for i, j in across])
    core = lax.ppermute(core, "az", inside + [(j, i) for i, j in inside])
    cost = [pl.CostEstimate(flops=n, bytes_accessed=n, transcendentals=0) for n in (10**3, 10**3)]
    own = call(own_kernel, OWN_OUTS, [VMEM], OWN_SCRATCH, cost_estimate=cost[0])(recv)
    up, down, up_power, down_power, pick_a, pick_b, value = own
    value = call(core_kernel, f32(PAIRS, 128), [VMEM] * 6, EDGE_SCRATCH, cost_estimate=cost[1])(
        core, down, down_power, pick_a, pick_b, value
    )
    result = call(chip_kernel, f32(2 * DEVS, 128), [VMEM] * 6, CHIP_SCRATCH)(
        chip, up, up_power, pick_a, pick_b, value
    )
    got = lax.all_to_all(result.reshape(DEVS, 2, 128), "acq", split_axis=0, concat_axis=0, tiled=True)
    outs = call(finish_kernel, (f32(32, 64),) * 3, [VMEM])(got.reshape(2 * DEVS, 128))
    return tuple(x.reshape(PAIR_DEV, 2, 64) for x in outs)


def solution(mesh):
    in_specs = (P("acq", "az", None), P("acq", "az", None), P("acq", None))
    out_specs = (P("acq", "az", None), P("acq", "az", None), P("acq", "az", None))
    return jax.shard_map(per_device, mesh=mesh, in_specs=in_specs, out_specs=out_specs, check_vma=False)
```

```python
import jax
import jax.numpy as jnp
from jax import lax
from jax.experimental import pallas as pl
from jax.experimental.pallas import tpu as pltpu
from jax.sharding import PartitionSpec as P

DEVS = 32
ACQ_DEV = 6
ACQ = DEVS * ACQ_DEV
PAIR_DEV = 16
PAIRS = DEVS * PAIR_DEV
ROWS = 10
HALF = 5
RG = 1280
STEP = 40
WIDE = STEP + 19
CHUNK = 60
K = 256
F32 = jnp.float32
BF16 = jnp.bfloat16
VMEM = pl.BlockSpec(memory_space=pltpu.VMEM)
HBM = pl.BlockSpec(memory_space=pltpu.HBM)
BIG = 3.38e38
PART = 8 * ACQ_DEV


def lanes_of(shape):
    return lax.broadcasted_iota(jnp.int32, shape, len(shape) - 1)


def odd_row():
    return lax.axis_index("az") & 1


def pack_kernel(re_hbm, im_hbm, pairs_hbm, chunks, re_ref, im_ref, pairs_ref, later, sems):
    odd = odd_row()
    copies = [
        pltpu.make_async_copy(source, target, sems.at[n])
        for n, (source, target) in enumerate(((pairs_hbm, pairs_ref), (re_hbm, re_ref), (im_hbm, im_ref)))
    ]
    for copy in copies:
        copy.start()
    lane = lanes_of((ACQ_DEV, 128))
    wide = lanes_of((3 * ACQ_DEV, 128))
    copies[0].wait()
    acq = pairs_ref[...]
    group = (acq * 171) >> 10
    local = (acq - ACQ_DEV * group) * 8 + (group & 7)
    order = lax.broadcasted_iota(jnp.int32, (2, PAIR_DEV), 0)
    index = (local + jnp.where(order == 0, 0, (group >> 3) * PART)).astype(F32)
    square = (PAIR_DEV, PAIR_DEV)
    diagonal = lax.broadcasted_iota(jnp.int32, square, 0) == lax.broadcasted_iota(jnp.int32, square, 1)
    columns = [
        jnp.sum(jnp.where(diagonal, jnp.broadcast_to(index[w : w + 1, :], square), 0.0), axis=1, keepdims=True)
        for w in range(2)
    ]
    none = jnp.zeros((3 * ACQ_DEV - PAIR_DEV, 128), F32)
    first, second = [jnp.concatenate([jnp.broadcast_to(x, (PAIR_DEV, 128)), none], axis=0) for x in columns]
    marks = jnp.where(wide == 60, first, jnp.where(wide == 61, second, 0.0))
    marks = [marks[n * ACQ_DEV : (n + 1) * ACQ_DEV] for n in range(3)]
    tiles = RG // 128
    for part, ref in enumerate((re_ref, im_ref)):
        copies[1 + part].wait()
        for r in range(HALF):
            row = r + HALF + odd * (9 - 2 * (r + HALF))
            for t in range(tiles):
                x = ref[row, :, t * 128 : (t + 1) * 128]
                later[part * HALF + r, :, t * 128 : (t + 1) * 128] = pltpu.roll(x, 64, 1)
    for d in range(DEVS):
        start = STEP * d - 10
        k = start // 128
        off = start - 128 * k
        spans = []
        for t, low, high in ((k, off, min(128, off + WIDE)), (k + 1, 0, off + WIDE - 128)):
            if low < high and 0 <= t < tiles:
                spans.append((t, False, low, high))
                shifted = [(low + 64, min(high + 64, 128)), (max(low + 64, 128) - 128, high + 64 - 128)]
                spans += [(t, True, x, y) for x, y in shifted if x < y]
        masks = [(lane >= low) & (lane < high) for _, _, low, high in spans]
        for part, ref in enumerate((re_ref, im_ref)):
            for r in range(HALF):
                row = r + odd * (9 - 2 * r)
                mixed = jnp.zeros((ACQ_DEV, 128), F32)
                for (t, shifted, _, _), mask in zip(spans, masks):
                    at = slice(t * 128, (t + 1) * 128)
                    mixed = jnp.where(mask, later[part * HALF + r, :, at] if shifted else ref[row, :, at], mixed)
                top = d * CHUNK + (part * HALF + r) * ACQ_DEV
                mixed = pltpu.roll(mixed, 128 - off, 1) if off else mixed
                if part == 0 and r < 3:
                    mixed = mixed + marks[r]
                chunks[top : top + ACQ_DEV, :] = mixed


def acq_rows(recv_ref, part, r):
    base = (part * HALF + r) * ACQ_DEV
    return jnp.concatenate(
        [recv_ref[pl.ds(base + a + 8 * g * CHUNK, 8, stride=CHUNK), :] for g in range(4) for a in range(ACQ_DEV)],
        axis=0,
    )


def chip_edge_kernel(recv_ref, out_ref):
    lane = lanes_of((ACQ, 128))
    for part in range(2):
        v0, v1 = [acq_rows(recv_ref, part, r) for r in (0, 1)]
        out_ref[part * ACQ : (part + 1) * ACQ, :] = jnp.where(lane < 64, v0, pltpu.roll(v1, 64, 1))
    out_ref[2 * ACQ :, :] = jnp.zeros((8, 128), F32)


def core_edge_kernel(recv_ref, out_ref):
    lane = lanes_of((ACQ, 128))
    for part in range(2):
        v3, v4 = [acq_rows(recv_ref, part, r) for r in (3, 4)]
        out_ref[part * ACQ : (part + 1) * ACQ, :] = jnp.where(lane < 64, pltpu.roll(v3, 64, 1), v4)


def pieces_of(x, count):
    out = []
    for n in range(count):
        piece = x.astype(BF16)
        out.append(piece)
        if n + 1 < count:
            x = x - piece.astype(F32)
    return out


def clamp(x):
    return jnp.minimum(jnp.maximum(x, -BIG), BIG)


def dot(x, y):
    return jnp.dot(x, y, preferred_element_type=F32)


def fill(table):
    for p in range(3):
        table[p * K + ACQ : (p + 1) * K, :] = jnp.zeros((K - ACQ, table.shape[1]), BF16)


def enter(table, x, at):
    for p, piece in enumerate(pieces_of(clamp(x), 3)):
        table[p * K : p * K + ACQ, at : at + x.shape[1]] = piece


def along_range():
    shape = (128, 128)
    k = lax.broadcasted_iota(jnp.int32, shape, 0)
    n = lax.broadcasted_iota(jnp.int32, shape, 1)
    c = n & 63
    first = jnp.where(c < STEP, c, jnp.where(c < STEP + 4, 10 + 20 * (c & 1), -1000))
    sample = k & 63
    inside = ((k >> 6) == (n >> 6)) & (sample >= first) & (sample <= first + 19)
    box = jnp.where(inside, 1.0, 0.0).astype(BF16)
    return jnp.concatenate([box, box], axis=0)


def choose(pick_a, pick_b, table, picked, at, width, parts):
    columns = slice(at, at + width)
    picked[PAIRS:, columns] = dot(pick_b[:, : parts * K], table[: parts * K, columns])
    for g in range(4):
        few = jnp.concatenate([table[p * K + g * PART : p * K + (g + 1) * PART, columns] for p in range(3)], axis=0)
        picked[128 * g : 128 * (g + 1), columns] = dot(pick_a[128 * g : 128 * (g + 1), : 3 * PART], few)


def cross(picked, top, count):
    fields = [[], []]
    for t in range(count):
        ra = picked[pl.ds(top, 16), t * 256 : t * 256 + 128]
        ia = picked[pl.ds(top, 16), t * 256 + 128 : t * 256 + 256]
        rb = picked[pl.ds(top + PAIRS, 16), t * 256 : t * 256 + 128]
        ib = picked[pl.ds(top + PAIRS, 16), t * 256 + 128 : t * 256 + 256]
        fields[0].append(ra * rb + ia * ib)
        fields[1].append(ia * rb - ra * ib)
    return fields


def own_rows(v):
    v0, v1, v2, v3, v4 = v
    low = lanes_of(v0.shape) < 64
    next_one = pltpu.roll(jnp.where(low, v4, v0), 64, 1)
    next_two = next_one + pltpu.roll(jnp.where(low, v3, v1), 64, 1)
    v12, v34 = v1 + v2, v3 + v4
    v012, v234 = v0 + v12, v2 + v34
    return [
        v012 + jnp.where(low, 0.0, next_two),
        (v012 + v3) + jnp.where(low, 0.0, next_one),
        v012 + v34,
        (v1 + v234) + jnp.where(low, next_one, 0.0),
        v234 + jnp.where(low, next_two, 0.0),
    ]


def edge_rows(near, far, edge, low):
    inside = (lanes_of(edge.shape) < 64) == low
    return near + jnp.where(inside, edge + pltpu.roll(edge, 64, 1), 0.0), far + jnp.where(inside, edge, 0.0)


def store_terms(terms, top, x):
    for n, piece in enumerate(pieces_of(x, 2)):
        terms[pl.ds(top, 16), n * 128 : (n + 1) * 128] = piece


def enter_power(table, x, box, at):
    high, mid, low = pieces_of(x, 3)
    enter(table, dot(jnp.concatenate([high, mid], axis=1), box) + dot(low, box[:128]), at)


def coherence_of(total, picked, top, row, at):
    x0 = total[pl.ds(top + 2 * row * PAIRS, 16), :]
    x1 = total[pl.ds(top + (2 * row + 1) * PAIRS, 16), :]
    wa = picked[pl.ds(top, 16), at : at + 128]
    wb = picked[pl.ds(top + PAIRS, 16), at : at + 128]
    inverse = lax.rsqrt(wa * wb + 1e-06)
    num = x0 * x0 + x1 * x1
    return num * lax.rsqrt(jnp.maximum(num, 1e-37)) * inverse, x0, x1, inverse


def for_pairs(body):
    def step(g, carry):
        body(pl.multiple_of(16 * g, 16))
        return carry

    lax.fori_loop(0, PAIRS // 16, step, 0, unroll=True)


def own_kernel(
    recv_ref, up_ref, down_ref, up_power, down_power, pick_a, pick_b, value_ref, table, picked, terms, total
):
    lane = lanes_of((128, K))
    few = lane - PART * ((lane * 342) >> 14)
    for g in range(4):
        head = jnp.concatenate([recv_ref[pl.ds(8 * g * CHUNK + p, 8, stride=CHUNK), :] for p in range(PAIR_DEV)], axis=0)
        rows = slice(128 * g, 128 * (g + 1))
        index = jnp.broadcast_to(head[:, 60:61], (128, K))
        pick_a[rows, :] = jnp.where(index == few.astype(F32), 1.0, 0.0).astype(BF16)
        index = jnp.broadcast_to(head[:, 61:62], (128, K))
        hot = jnp.where(index == lane.astype(F32), 1.0, 0.0).astype(BF16)
        for p in range(3):
            pick_b[rows, p * K : (p + 1) * K] = hot
    fill(table)
    box = along_range()
    squares = []
    for t in range(HALF):
        parts = [acq_rows(recv_ref, part, t) for part in range(2)]
        for part, x in enumerate(parts):
            enter(table, x, t * 256 + part * 128)
        squares.append(parts[0] * parts[0] + parts[1] * parts[1])
        choose(pick_a, pick_b, table, picked, t * 256, 256, 2)
    sums = own_rows(squares)
    up_power[:, 0:128], up_power[:, 128:256] = sums[0], sums[1]
    down_power[:, 0:128], down_power[:, 128:256] = sums[4], sums[3]
    enter_power(table, sums[2], box, HALF * 256)
    choose(pick_a, pick_b, table, picked, HALF * 256, 128, 3)

    def rows(top):
        for f, field in enumerate(cross(picked, top, HALF)):
            x = own_rows(field)
            here = pl.ds(top + f * PAIRS, 16)
            up_ref[here, 0:128], up_ref[here, 128:256] = x[0], x[1]
            down_ref[here, 0:128], down_ref[here, 128:256] = x[4], x[3]
            store_terms(terms, top + f * PAIRS, x[2])

    for_pairs(rows)
    total[...] = dot(terms[...], box)
    lane16 = lanes_of((16, 128)) & 63

    def some(top):
        size, x0, x1, inverse = coherence_of(total, picked, top, 0, HALF * 256)
        value_ref[pl.ds(top, 16), :] = jnp.where(lane16 < STEP, size, jnp.where(lane16 < STEP + 2, x0, x1) * inverse)

    for_pairs(some)


def edge_coherence(edge_ref, sums_ref, power_ref, pick_a, pick_b, table, picked, terms, total, low):
    fill(table)
    box = along_range()
    parts = [edge_ref[part * ACQ : (part + 1) * ACQ, :] for part in range(2)]
    for part, x in enumerate(parts):
        enter(table, x, part * 128)
    square = parts[0] * parts[0] + parts[1] * parts[1]
    for n, x in enumerate(edge_rows(power_ref[:, 0:128], power_ref[:, 128:256], square, low)):
        enter_power(table, x, box, 256 + n * 128)
    choose(pick_a, pick_b, table, picked, 0, 256, 2)
    choose(pick_a, pick_b, table, picked, 256, 256, 3)

    def rows(top):
        for f, field in enumerate(cross(picked, top, 1)):
            here = pl.ds(top + f * PAIRS, 16)
            for n, x in enumerate(edge_rows(sums_ref[here, 0:128], sums_ref[here, 128:256], field[0], low)):
                store_terms(terms, top + (2 * n + f) * PAIRS, x)

    for_pairs(rows)
    total[...] = dot(terms[...], box)


def edge_value(value_ref, total, picked, top):
    size = coherence_of(total, picked, top, 0, 256)[0] + coherence_of(total, picked, top, 1, 384)[0]
    return value_ref[pl.ds(top, 16), :] + jnp.where((lanes_of(size.shape) & 63) < STEP, size, 0.0)


def core_kernel(core_ref, sums_ref, power_ref, pick_a, pick_b, value_ref, out_ref, table, picked, terms, total):
    edge_coherence(core_ref, sums_ref, power_ref, pick_a, pick_b, table, picked, terms, total, False)

    def some(top):
        out_ref[pl.ds(top, 16), :] = edge_value(value_ref, total, picked, top)

    for_pairs(some)


def chip_kernel(chip_ref, sums_ref, power_ref, pick_a, pick_b, value_ref, out_ref, table, picked, terms, total, ends):
    edge_coherence(chip_ref, sums_ref, power_ref, pick_a, pick_b, table, picked, terms, total, True)

    def some(top):
        for p, piece in enumerate(pieces_of(edge_value(value_ref, total, picked, top), 3)):
            ends[pl.ds(top, 16), p * 128 : (p + 1) * 128] = piece

    for_pairs(some)

    n = lax.broadcasted_iota(jnp.int32, (128, 256), 0)
    m = lax.broadcasted_iota(jnp.int32, (128, 256), 1)
    c, j, o = n & 63, m >> 7, (m >> 5) & 3
    first = jnp.where(o == 0, 20 * j, jnp.where(o == 3, 1000, STEP - 2 + 2 * o + j))
    last = first + jnp.where(o == 0, 19, 0)
    same = ((n >> 6) == ((m & 1) ^ odd_row())) & (c >= first) & (c <= last)
    spread = jnp.where(same, 1.0, 0.0).astype(BF16)
    result = dot(ends[...], jnp.concatenate([spread] * 3, axis=0))
    owner = (lanes_of((8, 128)) >> 1) & 15
    for j in range(2):
        for g in range(4):
            out = None
            for p in range(PAIR_DEV):
                top = 128 * g + 8 * p
                rows_p = result[top : top + 8, j * 128 : (j + 1) * 128]
                out = rows_p if out is None else jnp.where(owner == p, rows_p, out)
            out_ref[pl.ds(16 * g + j, 8, stride=2), :] = out


def finish_kernel(got_ref, coh_ref, re_ref, im_ref):
    turned = jnp.transpose(got_ref[...])
    coh_ref[...] = turned[0:32] * 0.01
    re_ref[...] = turned[32:64]
    im_ref[...] = turned[64:96]


def call(kernel, outs, specs, scratch=(), limit=40, out_spec=VMEM, **more):
    return pl.pallas_call(
        kernel,
        out_shape=outs,
        in_specs=specs,
        out_specs=jax.tree.map(lambda _: out_spec, outs),
        scratch_shapes=[pltpu.VMEM(*x) if isinstance(x, tuple) else x for x in scratch],
        compiler_params=pltpu.CompilerParams(vmem_limit_bytes=limit * 1024 * 1024),
        **more,
    )


def f32(*shape):
    return jax.ShapeDtypeStruct(shape, F32)


def bf16(*shape):
    return jax.ShapeDtypeStruct(shape, BF16)


EDGE_OUTS = (f32(2 * PAIRS, 256),) * 2 + (f32(ACQ, 256),) * 2
OWN_OUTS = EDGE_OUTS + (bf16(PAIRS, K), bf16(PAIRS, 3 * K), f32(PAIRS, 128))
OWN_SCRATCH = (
    ((3 * K, HALF * 256 + 128), BF16),
    ((2 * PAIRS, HALF * 256 + 128), F32),
    ((2 * PAIRS, 256), BF16),
    ((2 * PAIRS, 128), F32),
)
EDGE_SCRATCH = (
    ((3 * K, 512), BF16),
    ((2 * PAIRS, 512), F32),
    ((4 * PAIRS, 256), BF16),
    ((4 * PAIRS, 128), F32),
)
CHIP_SCRATCH = EDGE_SCRATCH + (((PAIRS, 3 * 128), BF16),)


def per_device(slc_re, slc_im, pairs):
    send = call(
        pack_kernel,
        f32(DEVS * CHUNK, 128),
        [HBM] * 3,
        (
            ((ROWS, ACQ_DEV, RG), F32),
            ((ROWS, ACQ_DEV, RG), F32),
            ((2, PAIR_DEV), jnp.int32),
            ((2 * HALF, ACQ_DEV, RG), F32),
            pltpu.SemaphoreType.DMA((3,)),
        ),
        limit=40,
        out_spec=VMEM,
    )(*[pltpu.with_memory_space_constraint(x, pltpu.HBM) for x in (jnp.transpose(slc_re, (1, 0, 2)), jnp.transpose(slc_im, (1, 0, 2)), pairs.T)])
    send = send.reshape(DEVS, CHUNK // 4, 4, 128)
    recv = lax.all_to_all(send, "acq", split_axis=0, concat_axis=0, tiled=True)
    recv = recv.reshape(DEVS * CHUNK, 128)
    chip = call(chip_edge_kernel, f32(2 * ACQ + 8, 128), [VMEM])(recv)
    core = call(core_edge_kernel, f32(2 * ACQ, 128), [VMEM])(recv)
    count = lax.axis_size("az")
    across = [(i, i + 1) for i in range(1, count - 1, 2)]
    inside = [(i, i + 1) for i in range(0, count, 2)]
    chip = lax.ppermute(chip, "az", across + [(j, i) for i, j in across])
    core = lax.ppermute(core, "az", inside + [(j, i) for i, j in inside])
    cost = [pl.CostEstimate(flops=n, bytes_accessed=n, transcendentals=0) for n in (10**3, 10**3)]
    own = call(own_kernel, OWN_OUTS, [VMEM], OWN_SCRATCH, cost_estimate=cost[0])(recv)
    up, down, up_power, down_power, pick_a, pick_b, value = own
    value = call(core_kernel, f32(PAIRS, 128), [VMEM] * 6, EDGE_SCRATCH, cost_estimate=cost[1])(
        core, down, down_power, pick_a, pick_b, value
    )
    result = call(chip_kernel, f32(2 * DEVS, 128), [VMEM] * 6, CHIP_SCRATCH)(
        chip, up, up_power, pick_a, pick_b, value
    )
    got = lax.all_to_all(result.reshape(DEVS, 2, 128), "acq", split_axis=0, concat_axis=0, tiled=True)
    outs = call(finish_kernel, (f32(32, 64),) * 3, [VMEM])(got.reshape(2 * DEVS, 128))
    return tuple(x.reshape(PAIR_DEV, 2, 64) for x in outs)


def solution(mesh):
    in_specs = (P("acq", "az", None), P("acq", "az", None), P("acq", None))
    out_specs = (P("acq", "az", None), P("acq", "az", None), P("acq", "az", None))
    return jax.shard_map(per_device, mesh=mesh, in_specs=in_specs, out_specs=out_specs, check_vma=False)
```
